32 devices in a mesh: dp: 32 (over z, y, x, core).
Axes of the slice: x: 2, y: 2, z: 4, core: 2. Of those that a mesh axis runs over, the one named last changes fastest.
Arguments:
- tokens: bfloat16 [32, 1024, 768], P('dp'), may hold values from -6 to 6
- image_features: bfloat16 [32, 1024, 768], P('dp'), may hold values from -3 to 3
- segment_ids: int32 [32, 1024], P('dp'), may hold values from 0 to 7, never falling along the last dimension, each value on 1 to 512 neighbouring positions
- box_left: int32 [32, 1024], P('dp'), may hold values from 0 to 255
- box_top: int32 [32, 1024], P('dp'), may hold values from 0 to 255
- cotangent: bfloat16 [32, 1024, 768], P('dp'), may hold values from -6 to 6
- query_weight: bfloat16 [768, 768], P('dp'), may hold values from -0.21875 to 0.21875
- key_weight: bfloat16 [768, 768], P('dp'), may hold values from -0.21875 to 0.21875
- value_weight: bfloat16 [768, 768], P('dp'), may hold values from -0.21875 to 0.21875
- output_weight: bfloat16 [768, 768], P('dp'), may hold values from -0.625 to 0.625
- inner_weight: bfloat16 [768, 3072], P('dp'), may hold values from -0.21875 to 0.21875
- outer_weight: bfloat16 [3072, 768], P('dp'), may hold values from -0.109375 to 0.109375
- attention_gain: bfloat16 [768], P('dp'), may hold values from 0.25 to 1.75
- feed_gain: bfloat16 [768], P('dp'), may hold values from 0.25 to 1.75
- bias_tables: bfloat16 [1152], P('dp'), may hold values from -3 to 3
Outputs:
- layer_output: bfloat16 [32, 1024, 768], P('dp')
- input_gradient: float32 [32, 1024, 768], P('dp')
- query_gradient: float32 [768, 768], P('dp')
- key_gradient: float32 [768, 768], P('dp')
- value_gradient: float32 [768, 768], P('dp')
- projection_gradient: float32 [768, 768], P('dp')
- inner_gradient: float32 [768, 3072], P('dp')
- outer_gradient: float32 [3072, 768], P('dp')
- attention_gain_gradient: float32 [768], P('dp')
- feed_gain_gradient: float32 [768], P('dp')
- tables_gradient: float32 [1152], P('dp')
The draws below stay inside these ranges and needn't reach their ends.
Inputs may be any that keep to these rules, and one draw needn't show every extreme that they name: `segment_ids`: per row, never falling; each document has 1 to 512 tokens and one has exactly that many.
All inputs are finite; a program needn't handle non-finite values.
Results may differ from the reference program's by a relative error of at most 0.013.
Values may be sent and summed in bfloat16 or wider, within the bound.
No kernel may reach another device: no remote copies, remote signals or barrier semaphores. Data moves between devices by JAX's collectives and lax.ppermute only.
A program may use at most 384 MiB of HBM per device.

```python
import math
import jax
import jax.numpy as jnp
import numpy as np
from jax import lax

D = 768
HEADS = 12
HEAD_DIM = 64
FF = 3072
BUCKETS = 32
LENGTH = 1024
SEQS = 32


def set_ends(values, key, least, high):
    longest = values.shape.index(max(values.shape))
    spots = []
    for shift in (0, 1):
        where = [jax.random.randint(jax.random.fold_in(key, axis), (), 0, length) for axis, length in enumerate(values.shape)]
        where[longest] = (where[longest] + shift) % values.shape[longest]
        spots.append(tuple(where))
    return values.at[spots[0]].set(least).at[spots[1]].set(high)


def block_levels(rng, dims, pieces, smallest, top_value):
    def one(dim, parts):
        heights = jax.random.uniform(jax.random.fold_in(jax.random.fold_in(rng, 6), dim), (parts,), jnp.float32, smallest / len(pieces), top_value / len(pieces))
        return jnp.repeat(jnp.exp(heights), dims[dim] // parts).reshape((-1,) + (1,) * (len(dims) - dim - 1))

    level = one(*pieces[0])
    for cut in pieces[1:]:
        level = level * one(*cut)
    return level


def split_up(count, total, most, slope):
    weights = [(1 << 20) // math.isqrt(rank ** slope) + 1 for rank in range(2, count + 1)]
    spare, given = total - most - (count - 1), [1] * (count - 1)
    while spare > 0:
        free = [i for i in range(count - 1) if given[i] < most]
        pool, remaining = sum([weights[i] for i in free]), spare
        for i in free:
            addition = min(most - given[i], max(1, remaining * weights[i] // pool), spare)
            given[i] = given[i] + addition
            spare = spare - addition
    return np.array([most] + given)


def ragged(key, count, total, most, slope):
    if count == 2:
        one = jax.random.randint(key, (), max(1, total - most), min(most, total - 1) + 1)
        return jnp.stack([one, total - one])
    tallies = jnp.asarray(split_up(count, total, most, slope), jnp.int32)
    couples = (count - 1) // 2
    giver, receiver = tallies[1:1 + 2 * couples:2], tallies[2:2 + 2 * couples:2]
    margin = jnp.minimum(giver - 1, most - receiver)
    shifted = jax.random.randint(jax.random.fold_in(key, 1), (couples,), 0, 1 << 20) % (margin + 1)
    tallies = tallies.at[1:1 + 2 * couples:2].set(giver - shifted).at[2:2 + 2 * couples:2].set(receiver + shifted)
    return tallies[jax.random.permutation(jax.random.fold_in(key, 2), count)]


def scatter_about(key, shape, scale, most, shards=(), kind=jnp.bfloat16):
    factor_of = block_levels(key, shape, shards, -0.22, 0.18) if shards else 1.0
    entries = jax.random.normal(key, shape, jnp.float32) * scale * factor_of
    return jnp.minimum(jnp.maximum(entries, -most), most).astype(kind)


def setup_inputs(seed: int = 0) -> dict:
    arg_keys = jax.random.split(jax.random.key(seed), 16)
    tokens = scatter_about(arg_keys[0], (SEQS, LENGTH, D), 1.0, 6.0, ((0, 32),))
    image_features = scatter_about(arg_keys[1], (SEQS, LENGTH, D), 0.5, 3.0, ((0, 32),))
    segment_ids = jax.vmap(lambda own: jnp.searchsorted(jnp.cumsum(ragged(own, 8, LENGTH, LENGTH // 2, 2)), jnp.arange(LENGTH), side="right"))(jax.random.split(arg_keys[2], SEQS)).reshape((SEQS, LENGTH)).astype(jnp.int32)
    box_left = set_ends(jax.random.randint(arg_keys[3], (SEQS, LENGTH), 0, 256), jax.random.fold_in(arg_keys[3], 1), 0, 255).astype(jnp.int32)
    box_top = set_ends(jax.random.randint(arg_keys[4], (SEQS, LENGTH), 0, 256), jax.random.fold_in(arg_keys[4], 1), 0, 255).astype(jnp.int32)
    cotangent = scatter_about(arg_keys[5], (SEQS, LENGTH, D), 1.0, 6.0, ((0, 32),))
    query_weight = scatter_about(arg_keys[6], (D, D), D ** -0.5, 0.21875, ((0, 32),))
    key_weight = scatter_about(arg_keys[7], (D, D), D ** -0.5, 0.21875, ((0, 32),))
    value_weight = scatter_about(arg_keys[8], (D, D), D ** -0.5, 0.21875, ((0, 32),))
    output_weight = scatter_about(arg_keys[9], (D, D), (D // 8) ** -0.5, 0.625, ((0, 32),))
    inner_weight = scatter_about(arg_keys[10], (D, FF), D ** -0.5, 0.21875, ((0, 32),))
    outer_weight = scatter_about(arg_keys[11], (FF, D), FF ** -0.5, 0.109375, ((0, 32),))
    attention_gain = jnp.clip(1.0 + 0.15 * jax.random.normal(arg_keys[12], (D,), jnp.float32), 0.25, 1.75).astype(jnp.bfloat16)
    feed_gain = jnp.clip(1.0 + 0.15 * jax.random.normal(arg_keys[13], (D,), jnp.float32), 0.25, 1.75).astype(jnp.bfloat16)
    bias_tables = scatter_about(arg_keys[14], (3 * BUCKETS * HEADS,), 0.5, 3.0, ((0, 32),))
    return dict(tokens=tokens, image_features=image_features, segment_ids=segment_ids, box_left=box_left, box_top=box_top, cotangent=cotangent, query_weight=query_weight, key_weight=key_weight, value_weight=value_weight, output_weight=output_weight, inner_weight=inner_weight, outer_weight=outer_weight, attention_gain=attention_gain, feed_gain=feed_gain, bias_tables=bias_tables)


@jax.custom_vjp
def low(v):
    return lax.optimization_barrier(v.astype(jnp.bfloat16)).astype(jnp.float32)

@jax.custom_vjp
def low_back(v):
    return v

def low_keep(v):
    return (low(v), None)

def low_pass(kept, grad):
    return (grad,)

def back_keep(v):
    return (v, None)

def back_low(kept, grad):
    return (low(grad),)
low.defvjp(low_keep, low_pass)
low_back.defvjp(back_keep, back_low)
thresholds = (1, 2, 3, 4, 5, 6, 7, 8, 11, 16, 22, 32, 45, 64, 90)

def both(value):
    return low_back(low(value))

def bucket_of(offset):
    magnitude = jnp.zeros(offset.shape, jnp.int32)
    for limit in thresholds:
        magnitude = magnitude + (jnp.abs(offset) >= limit).astype(jnp.int32)
    return magnitude + BUCKETS // 2 * (offset > 0).astype(jnp.int32)

def scaled_norm(values, gain):
    return values * lax.rsqrt(lax.optimization_barrier(jnp.mean(values * values, axis=-1, keepdims=True)) + 1e-06) * gain

def one_row(start_x, segment_row, left_row, top_row, query_weight, key_weight, value_weight, output_weight, inner_weight, outer_weight, attention_gain, feed_gain, bias_tables):
    exact = lax.Precision.HIGHEST
    length = start_x.shape[0]
    head_size = D // HEADS
    normed_one = low(scaled_norm(start_x, attention_gain))

    def project(weight):
        return both(jnp.dot(normed_one, weight, precision=exact)).reshape(length, HEADS, head_size)
    queries = project(query_weight)
    keys = project(key_weight)
    values = project(value_weight)
    positions = jnp.arange(length, dtype=jnp.int32)
    table_three = bias_tables.reshape(3, BUCKETS, HEADS)
    bias = table_three[0][bucket_of(positions[None, :] - positions[:, None])]
    bias = bias + table_three[1][bucket_of(left_row[None, :] - left_row[:, None])]
    bias = bias + table_three[2][bucket_of(top_row[None, :] - top_row[:, None])]
    bias = jnp.transpose(bias, (2, 0, 1))
    scale = HEAD_DIM ** (-0.5)
    logits = jnp.einsum('ihd,jhd->hij', queries, keys, precision=exact) * scale + bias
    mask = segment_row[:, None] == segment_row[None, :]
    logits = low_back(jnp.where(mask[None], logits, -1e+30))
    probs = jax.nn.softmax(logits, axis=-1)
    attended = both(jnp.einsum('hij,jhd->ihd', low(probs), values, precision=exact)).reshape(length, D)
    middle = start_x + low_back(jnp.dot(attended, output_weight, precision=exact))
    normed_two = low(scaled_norm(middle, feed_gain))
    inner = low_back(jnp.dot(normed_two, inner_weight, precision=exact))
    activated = low(jax.nn.gelu(inner, approximate=True))
    return middle + low_back(jnp.dot(activated, outer_weight, precision=exact))

def reference(tokens, image_features, segment_ids, box_left, box_top, cotangent, query_weight, key_weight, value_weight, output_weight, inner_weight, outer_weight, attention_gain, feed_gain, bias_tables):
    start_x = tokens.astype(jnp.float32) + image_features.astype(jnp.float32)
    weights = tuple((item.astype(jnp.float32) for item in (query_weight, key_weight, value_weight, output_weight, inner_weight, outer_weight, attention_gain, feed_gain, bias_tables)))

    def forward(start_all, *weight_list):
        block = jax.checkpoint(one_row)

        def step(carry, items):
            return (carry, block(items[0], items[1], items[2], items[3], *weight_list))
        _, result = lax.scan(step, jnp.zeros((), jnp.float32), (start_all, segment_ids, box_left, box_top))
        return result
    result, pullback = jax.vjp(forward, start_x, *weights)
    grads = pullback(cotangent.astype(jnp.float32))
    return (result.astype(jnp.bfloat16), grads[0], grads[1], grads[2], grads[3], grads[4], grads[5], grads[6], grads[7], grads[8], grads[9])
```

```python
import functools

import numpy as np
import jax
import jax.numpy as jnp
from jax import lax
from jax.sharding import PartitionSpec as P
from jax.experimental import pallas as pl
from jax.experimental.pallas import tpu as pltpu

HEADS = 12
BUCKETS = 32
thresholds = (1, 2, 3, 4, 5, 6, 7, 8, 11, 16, 22, 32, 45, 64, 90)
COORDS = 256
TILE = 256
LANES = 128
AHEAD = 3
SMALL = pl.CostEstimate(flops=10**8, bytes_accessed=10**5, transcendentals=0)
F32 = jnp.float32
BF16 = jnp.bfloat16
NT = (((1,), (1,)), ((), ()))
NN = (((1,), (0,)), ((), ()))
TN = (((0,), (0,)), ((), ()))


def bucket_of(offset):
    magnitude = np.zeros(offset.shape, np.int32)
    for limit in thresholds:
        magnitude = magnitude + (np.abs(offset) >= limit).astype(np.int32)
    return magnitude + BUCKETS // 2 * (offset > 0).astype(np.int32)


def dot(left, right, dims=NN):
    return lax.dot_general(left, right, dims, preferred_element_type=F32)


def rows_of(tables):
    spot = np.arange(2 * TILE)
    signed = np.where(spot < TILE, spot, spot - 2 * TILE)
    marks = np.zeros((3, BUCKETS, 8, 2 * TILE), np.float32)
    picks = ((1, -signed), (2, -signed), (0, -signed), (0, TILE - signed), (0, -TILE - signed))
    for place, (table_index, offset) in enumerate(picks):
        marks[table_index, bucket_of(offset), place, spot] = 1.0
    marks = marks.reshape(3 * BUCKETS, 16 * TILE).astype(BF16)
    return dot(tables, jnp.asarray(marks), TN).reshape(HEADS, 8, 2 * TILE)


def bucket_marks():
    spot = np.arange(2 * TILE)
    falling = TILE - 1 - spot
    rising = spot - (TILE - 1)
    offsets = np.stack([falling, falling, rising, TILE + rising, rising - TILE], axis=1)
    marks = bucket_of(offsets)[:, :, None] == np.arange(LANES)
    return jnp.asarray(marks.astype(BF16).reshape(2 * TILE, 5 * LANES))


def toeplitz(row):
    wide = jnp.broadcast_to(row, (TILE, 2 * TILE))
    return pltpu.roll(wide, 0, axis=1, stride=1, stride_axis=0)[:, :TILE]


def skew_sum(square):
    wide = jnp.concatenate([square, jnp.zeros_like(square)], axis=1)
    return jnp.sum(pltpu.roll(wide, 0, axis=1, stride=1, stride_axis=0), axis=0, keepdims=True)


def one_hot_lanes(column, width):
    return (column == lax.broadcasted_iota(jnp.int32, (column.shape[0], width), 1)).astype(F32).astype(BF16)


def attend_kernel(qkv_ref, band_ref, seg_ref, seg_row, left_ref, top_ref, left_row, top_row, out_ref, probs_ref, sums_ref,
                key_side, query_side, position, marks):
    length = qkv_ref.shape[0]
    half = length // 2

    @pl.when(pl.program_id(0) == 0)
    def _():
        key_side[:, LANES:2 * LANES] = one_hot_lanes(seg_ref[...], LANES)
        key_side[:, 2 * LANES:2 * LANES + COORDS] = one_hot_lanes(left_ref[...], COORDS)
        key_side[:, 2 * LANES + COORDS:] = one_hot_lanes(top_ref[...], COORDS)
        down = lax.broadcasted_iota(jnp.int32, (LANES, length), 0)
        other = jnp.where(jnp.logical_and(down < 8, down != seg_row[...]), F32(-1e30), F32(0)).astype(BF16)
        query_side[0, LANES:2 * LANES, :] = other
        query_side[1, LANES:2 * LANES, :] = other
        down = lax.broadcasted_iota(jnp.int32, (COORDS, length), 0)
        marks[0] = (down == left_row[...]).astype(F32).astype(BF16)
        marks[1] = (down == top_row[...]).astype(F32).astype(BF16)
        query_side[0, 64:LANES, :] = jnp.zeros((64, length), BF16)
        query_side[1, :64, :] = jnp.zeros((64, length), BF16)

    key_side[:, :LANES] = qkv_ref[:, LANES:2 * LANES]
    values_across = qkv_ref[:, 2 * LANES:].T
    queries_across = qkv_ref[:, :LANES].T
    for h in range(2):
        bands = band_ref[h]
        own = slice(h * 64, (h + 1) * 64)
        query_side[h, own, :] = queries_across[own]
        for t in range(2):
            low = 2 * LANES + t * COORDS
            grid = toeplitz(bands[t:t + 1]).astype(BF16)
            query_side[h, low:low + COORDS, :] = dot(grid, marks[t]).astype(BF16)
        middle, below, above = (toeplitz(bands[t:t + 1]) for t in (2, 3, 4))
        position[h, :TILE, :TILE] = middle
        position[h, TILE:, TILE:] = middle
        position[h, TILE:, :TILE] = below
        position[h, :TILE, TILE:] = above

    def logits_of(block, tile, h):
        rows = slice(block * half, (block + 1) * half)
        here = slice(block * half + tile * TILE, block * half + (tile + 1) * TILE)
        return dot(key_side[rows, :], query_side[h, :, here]) + position[h, :, tile * TILE:(tile + 1) * TILE]

    def finish(block, tile, h, logits):
        rows = slice(block * half, (block + 1) * half)
        across = slice(tile * TILE, (tile + 1) * TILE)
        here = slice(block * half + tile * TILE, block * half + (tile + 1) * TILE)
        raised = jnp.exp(logits - jnp.max(logits, axis=0, keepdims=True))
        inverse = 1.0 / jnp.sum(raised, axis=0, keepdims=True)
        low = raised.astype(BF16)
        probs_ref[h, rows, across] = low
        sums_ref[h, :, here] = inverse
        return dot(values_across[h * 64:(h + 1) * 64, rows], low) * inverse

    jobs = [(block, tile, h) for block in range(2) for tile in range(half // TILE) for h in range(2)]
    pieces = {}

    def close(job, logits):
        block, tile, h = job
        pieces[job] = finish(*job, logits)
        if h == 1:
            here = slice(block * half + tile * TILE, block * half + (tile + 1) * TILE)
            out_ref[here, :] = jnp.concatenate([pieces[(block, tile, 0)], pieces[(block, tile, 1)]], axis=0).T.astype(BF16)

    waiting = []
    for job in jobs:
        waiting.append((job, logits_of(*job)))
        if len(waiting) > AHEAD:
            close(*waiting.pop(0))
    for item in waiting:
        close(*item)


def attend(packed, bands, seg, left, top):
    length, width = packed.shape[0], packed.shape[1] // 3
    pair = pl.BlockSpec((length, LANES), lambda g: (0, g))
    column = pl.BlockSpec((length, 1), lambda g: (0, 0))
    row = pl.BlockSpec((1, length), lambda g: (0, 0))
    return pl.pallas_call(
        attend_kernel,
        grid=(HEADS // 2,),
        in_specs=[
            pl.BlockSpec((length, 3 * LANES), lambda g: (0, g)),
            pl.BlockSpec((2, 8, 2 * TILE), lambda g: (g, 0, 0)),
            column, row, column, column, row, row,
        ],
        out_specs=[pair, pl.BlockSpec((2, length, length // 2), lambda g: (g, 0, 0)), pl.BlockSpec((2, 1, length), lambda g: (g, 0, 0))],
        out_shape=[
            jax.ShapeDtypeStruct((length, width), BF16),
            jax.ShapeDtypeStruct((HEADS, length, length // 2), BF16),
            jax.ShapeDtypeStruct((HEADS, 1, length), F32),
        ],
        scratch_shapes=[
            pltpu.VMEM((length, 2 * LANES + 2 * COORDS), BF16),
            pltpu.VMEM((2, 2 * LANES + 2 * COORDS, length), BF16),
            pltpu.VMEM((2, length // 2, length // 2), F32),
            pltpu.VMEM((2, COORDS, length), BF16),
        ],
        compiler_params=pltpu.CompilerParams(vmem_limit_bytes=56 * 1024 * 1024),
        cost_estimate=SMALL,
        name="attend",
    )(packed, bands, seg[:, None], seg[None], left[:, None], top[:, None], left[None], top[None])


def attend_back_kernel(first, qkv_ref, g_ref, probs_ref, inverse_ref, delta_ref, left_ref, top_ref, left_row, top_row, normed_ref,
                       bucket_ref, *rest):
    grad_ref, weight_ref, band_ref, key_across, marks, low_grads, spread, flip, normed_across = rest[-9:]
    length = g_ref.shape[0]
    half = length // 2
    step = pl.program_id(0)

    @pl.when(step == 0)
    def _():
        normed_across[...] = normed_ref[...].T
        marks[:, :COORDS] = one_hot_lanes(left_ref[...], COORDS)
        marks[:, COORDS:] = one_hot_lanes(top_ref[...], COORDS)
        down = COORDS - 1 - lax.broadcasted_iota(jnp.int32, (COORDS, length), 0)
        left_marks = (down == left_row[...]).astype(F32).astype(BF16)
        top_marks = (down == top_row[...]).astype(F32).astype(BF16)
        for h in range(2):
            key_across[h, 64:64 + COORDS, :] = left_marks
            key_across[h, 64 + COORDS:, :] = top_marks
        turned = TILE - 1 - lax.broadcasted_iota(jnp.int32, (TILE, TILE), 0)
        flip[...] = (turned == lax.broadcasted_iota(jnp.int32, (TILE, TILE), 1)).astype(F32).astype(BF16)

    keys_t = qkv_ref[:, LANES:2 * LANES].T
    upper = lax.broadcasted_iota(jnp.int32, (length, LANES), 1) >= LANES // 2
    zero = jnp.zeros((), BF16)
    inverse = jnp.concatenate([inverse_ref[0], inverse_ref[1], jnp.zeros((6, length), F32)], axis=0).T
    grads_h, across_h, queries_h, delta_h = [], [], [], []
    for h in range(2):
        key_across[h, :64, :] = keys_t[h * 64:(h + 1) * 64]
        own = upper == (h == 1)
        mine = jnp.where(own, g_ref[...].astype(F32) * inverse[:, h:h + 1], 0.0).astype(BF16)
        grads_h.append(mine)
        across_h.append(mine.T)
        queries_h.append(jnp.where(own, qkv_ref[:, :LANES], zero))
        delta_h.append(delta_ref[pl.ds(2 * (first + step) + h, 1), :] * inverse_ref[h])
    values = qkv_ref[:, 2 * LANES:]

    def spots(job):
        block, tile, h = job
        return (
            slice(block * half, (block + 1) * half),
            slice(block * half + tile * TILE, block * half + (tile + 1) * TILE),
            slice(tile * TILE, (tile + 1) * TILE),
        )

    def reach_of(job):
        rows, here, _ = spots(job)
        return dot(values[rows], across_h[job[2]][:, here])

    def push(job, reach):
        rows, here, across = spots(job)
        h = job[2]
        grads = (probs_ref[h, rows, across].astype(F32) * (reach - delta_h[h][:, here])).astype(BF16)
        low_grads[h, rows, across] = grads
        return dot(key_across[h, :, rows], grads)

    halves = {}

    def settle(job, both):
        block, tile, h = job
        rows, here, _ = spots(job)
        halves[job] = both[:64] * 0.125
        spread[h, :, here] = both[64:].astype(BF16)
        if h == 1:
            grad_ref[here, :LANES] = jnp.concatenate([halves[(block, tile, 0)], halves[job]], axis=0).T.astype(BF16)
        if h == 1 and tile == half // TILE - 1:
            grad_ref[rows, 2 * LANES:] = (
                dot(probs_ref[0, rows, :], grads_h[0][rows]) + dot(probs_ref[1, rows, :], grads_h[1][rows])
            ).astype(BF16)
            grad_ref[rows, LANES:2 * LANES] = (
                dot(low_grads[0, rows, :], queries_h[0][rows]) + dot(low_grads[1, rows, :], queries_h[1][rows])
            ).astype(BF16)

    jobs = [(block, tile, h) for block in range(2) for tile in range(half // TILE) for h in range(2)]
    reaching, pushed = [], []
    for job in jobs + [None] * 3:
        if job is not None:
            reaching.append((job, reach_of(job)))
        if reaching and (job is None or len(reaching) > 1):
            own, reach = reaching.pop(0)
            pushed.append((own, push(own, reach)))
        if pushed and (not reaching or len(pushed) > 1):
            settle(*pushed.pop(0))
    while reaching:
        own, reach = reaching.pop(0)
        pushed.append((own, push(own, reach)))
    while pushed:
        settle(*pushed.pop(0))

    weight_ref[...] = dot(normed_across[...], grad_ref[...]).astype(BF16)

    def part(h, block, down, tile):
        return low_grads[h, block * half + down * TILE:block * half + (down + 1) * TILE, tile * TILE:(tile + 1) * TILE].astype(F32)

    for h in range(2):
        squares = []
        for t in range(2):
            own = slice(t * COORDS, (t + 1) * COORDS)
            squares.append(dot(spread[h, own, :], marks[:, own]))
        for square in (
            (part(h, 0, 0, 0) + part(h, 0, 1, 1)) + (part(h, 1, 0, 0) + part(h, 1, 1, 1)),
            part(h, 0, 1, 0) + part(h, 1, 1, 0),
            part(h, 0, 0, 1) + part(h, 1, 0, 1),
        ):
            high = square.astype(BF16)
            low = (square - high.astype(F32)).astype(BF16)
            squares.append(dot(high, flip[...]) + dot(low, flip[...]))
        sums = [skew_sum(square) for square in squares]
        sums = jnp.concatenate(sums + [jnp.zeros_like(sums[0])] * 3, axis=0)
        high = sums.astype(BF16)
        both = dot(jnp.concatenate([high.astype(F32), sums - high.astype(F32)], axis=0).astype(BF16), bucket_ref[...])
        both = both[:8] + both[8:]
        picked = [both[t:t + 1, t * LANES:(t + 1) * LANES] for t in range(5)]
        band_ref[h] = jnp.concatenate(
            [picked[2] + picked[3] + picked[4], picked[0], picked[1], jnp.zeros((5, LANES), F32)], axis=0
        )


def attend_back(first, count, packed, grad_attended, probs, inverse, delta, left, top, normed, buckets, *deps):
    length, width = grad_attended.shape
    column = pl.BlockSpec((length, 1), lambda g: (0, 0))
    row = pl.BlockSpec((1, length), lambda g: (0, 0))
    return pl.pallas_call(
        functools.partial(attend_back_kernel, first),
        grid=(count,),
        in_specs=[
            pl.BlockSpec((length, 3 * LANES), lambda g: (0, first + g)),
            pl.BlockSpec((length, LANES), lambda g: (0, first + g)),
            pl.BlockSpec((2, length, length // 2), lambda g: (first + g, 0, 0)),
            pl.BlockSpec((2, 1, length), lambda g: (first + g, 0, 0)),
            pl.BlockSpec(delta.shape, lambda g: (0, 0)),
            column, column, row, row,
            pl.BlockSpec((length, width), lambda g: (0, 0)),
            pl.BlockSpec(buckets.shape, lambda g: (0, 0)),
        ] + [pl.BlockSpec(memory_space=pl.ANY)] * len(deps),
        out_specs=[
            pl.BlockSpec((length, 3 * LANES), lambda g: (0, g)),
            pl.BlockSpec((width, 3 * LANES), lambda g: (0, g)),
            pl.BlockSpec((2, 8, LANES), lambda g: (g, 0, 0)),
        ],
        out_shape=[
            jax.ShapeDtypeStruct((length, 3 * LANES * count), BF16),
            jax.ShapeDtypeStruct((width, 3 * LANES * count), BF16),
            jax.ShapeDtypeStruct((2 * count, 8, LANES), F32),
        ],
        scratch_shapes=[
            pltpu.VMEM((2, 64 + 2 * COORDS, length), BF16),
            pltpu.VMEM((length, 2 * COORDS), BF16),
            pltpu.VMEM((2, length, length // 2), BF16),
            pltpu.VMEM((2, 2 * COORDS, length), BF16),
            pltpu.VMEM((TILE, TILE), BF16),
            pltpu.VMEM((width, length), BF16),
        ],
        compiler_params=pltpu.CompilerParams(vmem_limit_bytes=56 * 1024 * 1024),
        cost_estimate=SMALL,
        name="attend_back",
    )(packed, grad_attended, probs, inverse, delta, left[:, None], top[:, None], left[None], top[None], normed, buckets, *deps)


ROOT = float(np.sqrt(2.0 / np.pi))


def feed_kernel(width, steps, kept, att_ref, start_ref, up_ref, inner_ref, outer_ref, output_ref, gain_ref,
                middle_ref, act_ref, back_ref, early_ref, late_ref, active, inner_back, normed, upstream):
    step = pl.program_id(0)
    parts = inner_ref.shape[1] // width

    @pl.when(step < steps)
    def _():
        size = att_ref.shape[0]
        rows = pl.ds(pl.multiple_of(step * size, size), size)
        up = up_ref[...]
        upstream[rows, :] = up
        middle = start_ref[...] + dot(att_ref[...], output_ref[...])
        middle_ref[...] = middle
        root = lax.rsqrt(jnp.mean(middle * middle, axis=1, keepdims=True) + 1e-06)
        low = (middle * root * gain_ref[...]).astype(BF16)
        normed[rows, :] = low

        def products(part):
            own = slice(part * width, (part + 1) * width)
            return dot(low, inner_ref[:, own]), dot(up, outer_ref[:, own], NT)

        def finish(part, point, reach):
            own = slice(part * width, (part + 1) * width)
            square = point * point
            bend = jnp.tanh(ROOT * point * (1.0 + 0.044715 * square))
            half = 0.5 + 0.5 * bend
            act = (point * half).astype(BF16)
            slope = half + (0.5 * ROOT) * point * (1.0 - bend * bend) * (1.0 + (3 * 0.044715) * square)
            grads = (slope * reach).astype(BF16)
            act_ref[:, own] = act
            back_ref[:, own] = grads
            active[rows, own] = act
            inner_back[rows, own] = grads

        held = products(0)
        for part in range(1, parts):
            following = products(part)
            finish(part - 1, *held)
            held = following
        finish(parts - 1, *held)

    @pl.when(jnp.logical_and(step >= steps, step < steps + parts))
    def _():
        own = pl.ds(pl.multiple_of((step - steps) * width, width), width)
        early_ref[...] = dot(active[:, own], upstream[...], TN).astype(BF16)

    def inner_grad():
        own = pl.ds(pl.multiple_of((step - steps - parts) * width, width), width)
        return dot(normed[...], inner_back[:, own], TN).astype(BF16)

    @pl.when(jnp.logical_and(step >= steps + parts, step < steps + parts + kept))
    def _():
        early_ref[...] = inner_grad()

    @pl.when(step >= steps + parts + kept)
    def _():
        late_ref[...] = inner_grad()


def weight_specs(width, parts, places):
    once = pl.Buffered(1)
    specs = [
        pl.BlockSpec((width, parts * width), lambda g: (0, 0), pipeline_mode=once),
        pl.BlockSpec((width, parts * width), lambda g: (0, 1), pipeline_mode=once),
        pl.BlockSpec((width, width), lambda g: (0, 2 * parts), pipeline_mode=once),
        pl.BlockSpec((1, width), lambda g: (0, 0)),
    ]
    return [specs[place] for place in places]


def feed(kept, attended, start, upstream, weights, gain):
    length, width = attended.shape
    steps = length // TILE
    parts = weights.shape[1] // width // 2
    rows = lambda g: (jnp.minimum(g, steps - 1), 0)
    tile = pl.BlockSpec((TILE, width), rows)
    broad = pl.BlockSpec((TILE, parts * width), rows)
    return pl.pallas_call(
        functools.partial(feed_kernel, width, steps, kept),
        grid=(steps + 2 * parts,),
        in_specs=[tile, tile, tile] + weight_specs(width, parts, (0, 1, 2, 3)),
        out_specs=[
            tile, broad, broad,
            pl.BlockSpec((width, width), lambda g: (0, jnp.clip(g - steps, 0, parts + kept - 1))),
            pl.BlockSpec((width, width), lambda g: (0, jnp.maximum(g - steps - parts - kept, 0))),
        ],
        out_shape=[
            jax.ShapeDtypeStruct((length, width), F32),
            jax.ShapeDtypeStruct((length, parts * width), BF16),
            jax.ShapeDtypeStruct((length, parts * width), BF16),
            jax.ShapeDtypeStruct((width, (parts + kept) * width), BF16),
            jax.ShapeDtypeStruct((width, (parts - kept) * width), BF16),
        ],
        scratch_shapes=[pltpu.VMEM((length, parts * width), BF16)] * 2 + [pltpu.VMEM((length, width), BF16)] * 2,
        compiler_params=pltpu.CompilerParams(vmem_limit_bytes=58 * 1024 * 1024),
        cost_estimate=SMALL,
        name="feed",
    )(attended, start, upstream, weights, weights, weights, gain)


def feed_back_kernel(width, steps, att_ref, middle_ref, up_ref, act_ref, back_ref, inner_ref, outer_ref, output_ref, gain_ref,
                     *rest):
    layer_ref, out_ref, seen_ref, delta_ref, weight_ref, low_middle, attended = rest[-7:]
    step = pl.program_id(0)

    @pl.when(step < steps)
    def _():
        size = att_ref.shape[0]
        rows = pl.ds(pl.multiple_of(step * size, size), size)
        att = att_ref[...]
        attended[rows, :] = att
        gain = gain_ref[...]
        middle = middle_ref[...]
        back = dot(back_ref[...], inner_ref[...], NT)
        result = middle
        for part in range(act_ref.shape[1] // width):
            own = slice(part * width, (part + 1) * width)
            result = result + dot(act_ref[:, own], outer_ref[:, own])
        root = lax.rsqrt(jnp.mean(middle * middle, axis=1, keepdims=True) + 1e-06)
        scaled = middle * root
        slant = jnp.mean(back * scaled * gain, axis=1, keepdims=True)
        grad_middle = up_ref[...].astype(F32) + root * (gain * back - scaled * slant)
        out_ref[...] = grad_middle
        rounded = grad_middle.astype(BF16)
        low_middle[rows, :] = rounded
        layer_ref[...] = result.astype(BF16)
        seen = dot(rounded, output_ref[...], NT).astype(BF16)
        seen_ref[...] = seen
        product = att.astype(F32) * seen.astype(F32)
        high = product.astype(BF16)
        low = (product - high.astype(F32)).astype(BF16)
        head = lax.broadcasted_iota(jnp.int32, (16, width), 0)
        lane = lax.broadcasted_iota(jnp.int32, (16, width), 1)
        marks = jnp.logical_and(lane >= head * 64, lane < head * 64 + 64).astype(F32).astype(BF16)
        delta_ref[...] = dot(marks, high, NT) + dot(marks, low, NT)

    @pl.when(step == steps)
    def _():
        weight_ref[...] = dot(attended[...], low_middle[...], TN).astype(BF16)


def feed_back(attended, middle, upstream, act, back, weights, gain, *deps):
    length, width = attended.shape
    steps = length // TILE
    parts = weights.shape[1] // width // 2
    rows = lambda g: (jnp.minimum(g, steps - 1), 0)
    tile = pl.BlockSpec((TILE, width), rows)
    broad = pl.BlockSpec((TILE, parts * width), rows)
    tokens = jax.ShapeDtypeStruct((length, width), BF16)
    return pl.pallas_call(
        functools.partial(feed_back_kernel, width, steps),
        grid=(steps + 1,),
        in_specs=[tile, tile, tile, broad, broad] + weight_specs(width, parts, (0, 1, 2, 3))
        + [pl.BlockSpec(memory_space=pl.ANY)] * len(deps),
        out_specs=[
            tile, tile, tile,
            pl.BlockSpec((16, TILE), lambda g: (0, jnp.minimum(g, steps - 1))),
            pl.BlockSpec((width, width), lambda g: (0, 0)),
        ],
        out_shape=[
            tokens,
            jax.ShapeDtypeStruct((length, width), F32),
            tokens,
            jax.ShapeDtypeStruct((16, length), F32),
            jax.ShapeDtypeStruct((width, width), BF16),
        ],
        scratch_shapes=[pltpu.VMEM((length, width), BF16)] * 2,
        compiler_params=pltpu.CompilerParams(vmem_limit_bytes=56 * 1024 * 1024),
        cost_estimate=SMALL,
        name="feed_back",
    )(attended, middle, upstream, act, back, weights, weights, weights, gain, *deps)


def last_kernel(start_ref, middle_ref, gain_ref, weight_ref, *rest):
    grads_refs, out_ref = rest[:2], rest[-1]
    start = start_ref[...]
    gain = gain_ref[...]
    root = lax.rsqrt(jnp.mean(start * start, axis=1, keepdims=True) + 1e-06)
    scaled = start * root
    low = 0
    back = 0.0
    for grads_ref in grads_refs:
        high = low + grads_ref.shape[1]
        back = back + dot(grads_ref[...], weight_ref[:, low:high], NT)
        low = high
    slant = jnp.mean(back * scaled * gain, axis=1, keepdims=True)
    out_ref[...] = middle_ref[...] + root * (gain * back - scaled * slant)


def last(start, middle, gain, weights, grads, *deps):
    length, width = start.shape
    tile = pl.BlockSpec((TILE, width), lambda g: (g, 0))
    total = sum(item.shape[1] for item in grads)
    return pl.pallas_call(
        last_kernel,
        grid=(length // TILE,),
        in_specs=[
            tile, tile, pl.BlockSpec((1, width), lambda g: (0, 0)),
            pl.BlockSpec((width, total), lambda g: (0, 0), pipeline_mode=pl.Buffered(1)),
        ]
        + [pl.BlockSpec((TILE, item.shape[1]), lambda g: (g, 0)) for item in grads]
        + [pl.BlockSpec(memory_space=pl.ANY)] * len(deps),
        out_specs=tile,
        out_shape=jax.ShapeDtypeStruct((length, width), F32),
        compiler_params=pltpu.CompilerParams(vmem_limit_bytes=40 * 1024 * 1024),
        cost_estimate=SMALL,
        name="last",
    )(start, middle, gain, weights, *grads, *deps)


def half_kernel(count, core_ref, *refs):
    out_ref = refs[-1]
    low = 0
    for array_ref in refs[:count]:
        high = low + array_ref.shape[-1]
        for place in range(array_ref.shape[0]):
            out_ref[0, place, :, low:high] = array_ref[place, 0, 0]
        low = high


def merge_kernel(count, core_ref, *refs):
    came_ref, out_ref = refs[count], refs[-1]
    low = 0
    for array_ref in refs[:count]:
        high = low + array_ref.shape[-1]
        for place in range(array_ref.shape[0]):
            out_ref[0, place, :, low:high] = (
                array_ref[place, 0, 0].astype(F32) + came_ref[0, place, :, low:high].astype(F32)
            ).astype(BF16)
        low = high


def core_part(kernel, core, arrays, owned, came, *deps):
    outer = arrays[0].shape[0] // owned // 8
    width = sum(array.shape[1] for array in arrays)
    block = pl.BlockSpec((1, outer, owned, width), lambda g, core: (g, 0, 0, 0))
    return pl.pallas_call(
        functools.partial(kernel, len(arrays)),
        grid_spec=pltpu.PrefetchScalarGridSpec(
            num_scalar_prefetch=1,
            grid=(4,),
            in_specs=[
                pl.BlockSpec((outer, 1, 1, owned, array.shape[1]), lambda g, core: (0, g, core[0], 0, 0)) for array in arrays
            ]
            + [block] * len(came) + [pl.BlockSpec(memory_space=pl.ANY)] * len(deps),
            out_specs=block,
        ),
        out_shape=jax.ShapeDtypeStruct((4, outer, owned, width), BF16),
        compiler_params=pltpu.CompilerParams(vmem_limit_bytes=40 * 1024 * 1024),
        cost_estimate=SMALL,
        name="core_part",
    )(core, *[array.reshape(outer, 4, 2, owned, array.shape[1]) for array in arrays], *came, *deps)


def fold_kernel(array_ref, *rest):
    out_ref = rest[-1]
    for place in range(array_ref.shape[0]):
        out_ref[0, place] = array_ref[place, 0]


def fold(array, *deps):
    inner, outer, owned, width = array.shape
    return pl.pallas_call(
        fold_kernel,
        grid=(outer,),
        in_specs=[pl.BlockSpec((inner, 1, owned, width), lambda g: (0, g, 0, 0))] + [pl.BlockSpec(memory_space=pl.ANY)] * len(deps),
        out_specs=pl.BlockSpec((1, inner, owned, width), lambda g: (g, 0, 0, 0)),
        out_shape=jax.ShapeDtypeStruct((outer, inner, owned, width), BF16),
        compiler_params=pltpu.CompilerParams(vmem_limit_bytes=40 * 1024 * 1024),
        cost_estimate=SMALL,
        name="fold",
    )(array, *deps)


def gather_sum_kernel(array_ref, *rest):
    out_ref = rest[-1]
    total = array_ref[0].astype(F32)
    for place in range(1, array_ref.shape[0]):
        total = total + array_ref[place].astype(F32)
    out_ref[...] = total.astype(out_ref.dtype)


def gather_sum(array, *deps):
    inner, outer, owned, width = array.shape
    return pl.pallas_call(
        gather_sum_kernel,
        grid=(outer,),
        in_specs=[pl.BlockSpec((inner, 1, owned, width), lambda g: (0, g, 0, 0))] + [pl.BlockSpec(memory_space=pl.ANY)] * len(deps),
        out_specs=pl.BlockSpec((1, owned, width), lambda g: (g, 0, 0)),
        out_shape=jax.ShapeDtypeStruct((outer, owned, width), BF16),
        compiler_params=pltpu.CompilerParams(vmem_limit_bytes=40 * 1024 * 1024),
        cost_estimate=SMALL,
        name="gather_sum",
    )(array, *deps)


def weave_kernel(core_ref, own_ref, came_ref, out_ref):
    core = core_ref[0]
    for place in range(own_ref.shape[1]):
        out_ref[0, place, core] = own_ref[0, place]
        out_ref[0, place, 1 - core] = came_ref[0, place]


def weave(core, own, came):
    outer, inner, owned, width = own.shape
    block = pl.BlockSpec((1, inner, owned, width), lambda g, core: (g, 0, 0, 0))
    return pl.pallas_call(
        weave_kernel,
        grid_spec=pltpu.PrefetchScalarGridSpec(
            num_scalar_prefetch=1,
            grid=(outer,),
            in_specs=[block, block],
            out_specs=pl.BlockSpec((1, inner, 2, owned, width), lambda g, core: (g, 0, 0, 0, 0)),
        ),
        out_shape=jax.ShapeDtypeStruct((outer, inner, 2, owned, width), BF16),
        compiler_params=pltpu.CompilerParams(vmem_limit_bytes=40 * 1024 * 1024),
        cost_estimate=SMALL,
        name="weave",
    )(core, own, came)


def turn(array, shift):
    return lax.dynamic_slice_in_dim(jnp.concatenate([array, array], axis=0), shift, array.shape[0], axis=0)


def long_start(segments):
    names = jnp.arange(8, dtype=jnp.int32)
    counts = jnp.sum((segments[None, :] == names[:, None]).astype(jnp.int32), axis=1)
    return jnp.sum((segments < jnp.argmax(counts).astype(jnp.int32)).astype(jnp.int32))


def member_groups(members, low, high):
    apart = 1 << low
    span = 1 << high
    return [
        [base + apart * place for place in range(span // apart)]
        for base in range(members)
        if (base & (span - 1) & ~(apart - 1)) == 0
    ]


def swap_cores(members, array):
    return lax.ppermute(array, "dp", [(place, place ^ 1) for place in range(members)])


def across_plane(members, array):
    return lax.all_to_all(array, "dp", 0, 0, axis_index_groups=member_groups(members, 1, 3))


def along_line(members, array):
    level = lax.all_to_all(
        array, "dp", 0, 0, axis_index_groups=member_groups(members, 3, members.bit_length() - 1)
    )
    return jnp.sum(level.astype(F32), axis=0)


def gather_rows(members, core, array, *deps):
    owned, width = array.shape
    outer = members // 8
    level = lax.all_to_all(
        jnp.broadcast_to(array[None], (outer, owned, width)), "dp", 0, 0,
        axis_index_groups=member_groups(members, 3, members.bit_length() - 1),
    )
    level = lax.all_to_all(
        jnp.broadcast_to(level[None], (4, outer, owned, width)), "dp", 0, 0,
        axis_index_groups=member_groups(members, 1, 3),
    )
    level = fold(level, *deps)
    return weave(core, level, swap_cores(members, level)).reshape(members * owned, width)


def per_device(
    members,
    tokens,
    image_features,
    segment_ids,
    box_left,
    box_top,
    cotangent,
    query_weight,
    key_weight,
    value_weight,
    output_weight,
    inner_weight,
    outer_weight,
    attention_gain,
    feed_gain,
    bias_tables,
):
    length, width = tokens.shape[1:]
    owned = query_weight.shape[0]
    parts = inner_weight.shape[1] // width
    spots = bias_tables.shape[0]

    small = jnp.concatenate(
        [
            attention_gain[:, None],
            feed_gain[:, None],
            jnp.pad(bias_tables, (0, 2 * owned - spots)).reshape(owned, 2),
            jnp.zeros((owned, LANES - 4), BF16),
        ],
        axis=1,
    )
    pairs = width // LANES
    trio = jnp.concatenate([query_weight, key_weight, value_weight], axis=1)
    trio = trio.reshape(owned, 3, pairs, LANES).transpose(0, 2, 1, 3).reshape(owned, 3 * width)
    core = (lax.axis_index("dp") & 1).reshape(1)
    inner_own = inner_weight.reshape(owned, width, parts).transpose(0, 2, 1).reshape(owned, parts * width)
    second = lax.all_gather(
        jnp.concatenate([inner_own, outer_weight.reshape(owned, parts * width), output_weight], axis=1),
        "dp", axis=0, tiled=True,
    )
    shift = long_start(segment_ids[0])
    segments, left, top = (turn(item[0], shift) for item in (segment_ids, box_left, box_top))
    start = turn(tokens[0], shift).astype(F32) + turn(image_features[0], shift).astype(F32)
    upstream = turn(cotangent[0], shift)
    root = lax.rsqrt(jnp.mean(start * start, axis=1, keepdims=True) + 1e-06)
    little = gather_rows(members, core, small)
    gain_one = little[:, 0].astype(F32)[None]
    gain_two = little[:, 1].astype(F32)[None]
    bands = rows_of(little[:, 2:4].reshape(-1, 2 * owned)[:, :spots].reshape(3 * BUCKETS, HEADS))
    project = gather_rows(
        members, core, trio, start, upstream, root, segments, left, top, gain_one, gain_two, bands, little
    )
    normed = (start * root * gain_one).astype(BF16)
    scale = jnp.where(jnp.arange(3 * width) % (3 * LANES) < LANES, 0.125, 1.0)[None]
    packed = (dot(normed, project) * scale).astype(BF16)
    attended, probs, inverse = attend(packed, bands, segments, left, top)

    middle, act, inner_back, outer_grad, inner_grad = feed(0, attended, start, upstream, second, gain_two)
    outer_sum = lax.psum_scatter(outer_grad, "dp", scatter_dimension=0, tiled=True)
    sent = core_part(half_kernel, 1 - core, [inner_grad], owned, [])
    inner_one = core_part(merge_kernel, core, [inner_grad], owned, [swap_cores(members, sent)])
    inner_two = across_plane(members, inner_one)

    layer, grad_middle, grad_attended, delta, output_grad = feed_back(
        attended, middle, upstream, act, inner_back, second, gain_two, inner_one
    )
    inner_two = gather_sum(inner_two, delta)
    inner_last = along_line(members, inner_two)

    split = pairs - pairs // 3
    buckets = bucket_marks()
    grads_a, weights_a, bands_a = attend_back(
        0, split, packed, grad_attended, probs, inverse, delta, left, top, normed, buckets, inner_two
    )
    group = [output_grad, weights_a]
    sent = core_part(half_kernel, 1 - core, group, owned, [], inner_last)
    first_one = core_part(merge_kernel, core, group, owned, [swap_cores(members, sent)])
    first_two = across_plane(members, first_one)
    grads_b, weights_b, bands_b = attend_back(
        split, pairs - split, packed, grad_attended, probs, inverse, delta, left, top, normed, buckets, first_one
    )
    first_two = gather_sum(first_two, bands_b)
    first_last = along_line(members, first_two)

    tables_grad = jnp.concatenate([bands_a, bands_b], axis=0)[:, :3, :BUCKETS].transpose(1, 2, 0).reshape(-1)
    room = -(-tables_grad.size // owned // LANES) * LANES
    tables_grad = jnp.pad(tables_grad, (0, owned * room - tables_grad.size)).astype(BF16).reshape(1, owned, room)
    tables_grad = jnp.broadcast_to(tables_grad, (members, owned, room)).reshape(width, room)
    group = [weights_b, tables_grad]
    sent = core_part(half_kernel, 1 - core, group, owned, [], first_two)
    second_one = core_part(merge_kernel, core, group, owned, [swap_cores(members, sent)])
    second_two = across_plane(members, second_one)
    input_gradient = last(start, grad_middle, gain_one, project, [grads_a, grads_b], second_one)
    second_two = gather_sum(second_two, input_gradient)
    second_last = along_line(members, second_two)
    tables_last = lax.dynamic_slice_in_dim(
        second_last[:, weights_b.shape[1]:].reshape(-1), lax.axis_index("dp") * spots, spots
    )
    outer_sum = outer_sum.astype(F32)
    edge = width
    trio_last = jnp.concatenate([first_last[:, edge:], second_last[:, :weights_b.shape[1]]], axis=1)
    gain_grad = jnp.sum(trio.astype(F32) * trio_last, axis=1) / attention_gain.astype(F32)
    trio_last = trio_last.reshape(owned, pairs, 3, LANES)
    inner_sum = inner_last.reshape(owned, parts, width).transpose(0, 2, 1).reshape(owned, parts * width)
    feed_gain_grad = jnp.sum(inner_weight.astype(F32) * inner_sum, axis=1) / feed_gain.astype(F32)
    return (
        turn(layer, length - shift)[None],
        turn(input_gradient, length - shift)[None],
        trio_last[:, :, 0].reshape(owned, width),
        trio_last[:, :, 1].reshape(owned, width),
        trio_last[:, :, 2].reshape(owned, width),
        first_last[:, :width],
        inner_sum,
        outer_sum.reshape(outer_weight.shape),
        gain_grad,
        feed_gain_grad,
        tables_last,
    )


def solution(mesh):
    rows = P("dp", None)
    cubes = P("dp", None, None)
    line = P("dp")
    return jax.shard_map(
        functools.partial(per_device, mesh.shape["dp"]),
        mesh=mesh,
        in_specs=(cubes, cubes, rows, rows, rows, cubes) + (rows,) * 6 + (line,) * 3,
        out_specs=(cubes, cubes) + (rows,) * 6 + (line,) * 3,
        check_vma=False,
    )
```

```python
import functools

import numpy as np
import jax
import jax.numpy as jnp
from jax import lax
from jax.sharding import PartitionSpec as P
from jax.experimental import pallas as pl
from jax.experimental.pallas import tpu as pltpu

HEADS = 12
BUCKETS = 32
thresholds = (1, 2, 3, 4, 5, 6, 7, 8, 11, 16, 22, 32, 45, 64, 90)
COORDS = 256
TILE = 256
LANES = 128
AHEAD = 3
SMALL = pl.CostEstimate(flops=10**8, bytes_accessed=10**5, transcendentals=0)
F32 = jnp.float32
BF16 = jnp.bfloat16
NT = (((1,), (1,)), ((), ()))
NN = (((1,), (0,)), ((), ()))
TN = (((0,), (0,)), ((), ()))


def bucket_of(offset):
    magnitude = np.zeros(offset.shape, np.int32)
    for limit in thresholds:
        magnitude = magnitude + (np.abs(offset) >= limit).astype(np.int32)
    return magnitude + BUCKETS // 2 * (offset > 0).astype(np.int32)


def dot(left, right, dims=NN):
    return lax.dot_general(left, right, dims, preferred_element_type=F32)


def rows_of(tables):
    spot = np.arange(2 * TILE)
    signed = np.where(spot < TILE, spot, spot - 2 * TILE)
    marks = np.zeros((3, BUCKETS, 8, 2 * TILE), np.float32)
    picks = ((1, -signed), (2, -signed), (0, -signed), (0, TILE - signed), (0, -TILE - signed))
    for place, (table_index, offset) in enumerate(picks):
        marks[table_index, bucket_of(offset), place, spot] = 1.0
    marks = marks.reshape(3 * BUCKETS, 16 * TILE).astype(BF16)
    return dot(tables, jnp.asarray(marks), TN).reshape(HEADS, 8, 2 * TILE)


def bucket_marks():
    spot = np.arange(2 * TILE)
    falling = TILE - 1 - spot
    rising = spot - (TILE - 1)
    offsets = np.stack([falling, falling, rising, TILE + rising, rising - TILE], axis=1)
    marks = bucket_of(offsets)[:, :, None] == np.arange(LANES)
    return jnp.asarray(marks.astype(BF16).reshape(2 * TILE, 5 * LANES))


def toeplitz(row):
    wide = jnp.broadcast_to(row, (TILE, 2 * TILE))
    return pltpu.roll(wide, 0, axis=1, stride=1, stride_axis=0)[:, :TILE]


def skew_sum(square):
    wide = jnp.concatenate([square, jnp.zeros_like(square)], axis=1)
    return jnp.sum(pltpu.roll(wide, 0, axis=1, stride=1, stride_axis=0), axis=0, keepdims=True)


def one_hot_lanes(column, width):
    return (column == lax.broadcasted_iota(jnp.int32, (column.shape[0], width), 1)).astype(F32).astype(BF16)


def attend_kernel(qkv_ref, band_ref, seg_ref, seg_row, left_ref, top_ref, left_row, top_row, out_ref, probs_ref, sums_ref,
                key_side, query_side, position, marks):
    length = qkv_ref.shape[0]
    half = length // 2

    @pl.when(pl.program_id(0) == 0)
    def _():
        key_side[:, LANES:2 * LANES] = one_hot_lanes(seg_ref[...], LANES)
        key_side[:, 2 * LANES:2 * LANES + COORDS] = one_hot_lanes(left_ref[...], COORDS)
        key_side[:, 2 * LANES + COORDS:] = one_hot_lanes(top_ref[...], COORDS)
        down = lax.broadcasted_iota(jnp.int32, (LANES, length), 0)
        other = jnp.where(jnp.logical_and(down < 8, down != seg_row[...]), F32(-1e30), F32(0)).astype(BF16)
        query_side[0, LANES:2 * LANES, :] = other
        query_side[1, LANES:2 * LANES, :] = other
        down = lax.broadcasted_iota(jnp.int32, (COORDS, length), 0)
        marks[0] = (down == left_row[...]).astype(F32).astype(BF16)
        marks[1] = (down == top_row[...]).astype(F32).astype(BF16)
        query_side[0, 64:LANES, :] = jnp.zeros((64, length), BF16)
        query_side[1, :64, :] = jnp.zeros((64, length), BF16)

    key_side[:, :LANES] = qkv_ref[:, LANES:2 * LANES]
    values_across = qkv_ref[:, 2 * LANES:].T
    queries_across = qkv_ref[:, :LANES].T
    for h in range(2):
        bands = band_ref[h]
        own = slice(h * 64, (h + 1) * 64)
        query_side[h, own, :] = queries_across[own]
        middle, below, above = (toeplitz(bands[t:t + 1]) for t in (2, 3, 4))
        position[h, :TILE, :TILE] = middle
        position[h, TILE:, TILE:] = middle
        position[h, TILE:, :TILE] = below
        position[h, :TILE, TILE:] = above

    for t in range(2):
        low = 2 * LANES + t * COORDS
        grids = jnp.concatenate([toeplitz(band_ref[h, t:t + 1]) for h in range(2)], axis=0).astype(BF16)
        spread = dot(grids, marks[t]).astype(BF16)
        for h in range(2):
            query_side[h, low:low + COORDS, :] = spread[h * COORDS:(h + 1) * COORDS]

    def logits_of(block, tile, h):
        rows = slice(block * half, (block + 1) * half)
        here = slice(block * half + tile * TILE, block * half + (tile + 1) * TILE)
        return dot(key_side[rows, :], query_side[h, :, here]) + position[h, :, tile * TILE:(tile + 1) * TILE]

    def finish(block, tile, h, logits):
        rows = slice(block * half, (block + 1) * half)
        across = slice(tile * TILE, (tile + 1) * TILE)
        here = slice(block * half + tile * TILE, block * half + (tile + 1) * TILE)
        raised = jnp.exp(logits - jnp.max(logits, axis=0, keepdims=True))
        inverse = 1.0 / jnp.sum(raised, axis=0, keepdims=True)
        low = raised.astype(BF16)
        probs_ref[h, rows, across] = low
        sums_ref[h, :, here] = inverse
        return dot(values_across[h * 64:(h + 1) * 64, rows], low) * inverse

    jobs = [(block, tile, h) for block in range(2) for tile in range(half // TILE) for h in range(2)]
    pieces = {}

    def close(job, logits):
        block, tile, h = job
        pieces[job] = finish(*job, logits)
        if h == 1:
            here = slice(block * half + tile * TILE, block * half + (tile + 1) * TILE)
            out_ref[here, :] = jnp.concatenate([pieces[(block, tile, 0)], pieces[(block, tile, 1)]], axis=0).T.astype(BF16)

    waiting = []
    for job in jobs:
        waiting.append((job, logits_of(*job)))
        if len(waiting) > AHEAD:
            close(*waiting.pop(0))
    for item in waiting:
        close(*item)


def attend(packed, bands, seg, left, top, columns):
    length, width = packed.shape[0], packed.shape[1] // 3
    pair = pl.BlockSpec((length, LANES), lambda g: (0, g))
    column = pl.BlockSpec((length, 1), lambda g: (0, 0))
    row = pl.BlockSpec((1, length), lambda g: (0, 0))
    return pl.pallas_call(
        attend_kernel,
        grid=(HEADS // 2,),
        in_specs=[
            pl.BlockSpec((length, 3 * LANES), lambda g: (0, g)),
            pl.BlockSpec((2, 8, 2 * TILE), lambda g: (g, 0, 0)),
            column, row, column, column, row, row,
        ],
        out_specs=[pair, pl.BlockSpec((2, length, length // 2), lambda g: (g, 0, 0)), pl.BlockSpec((2, 1, length), lambda g: (g, 0, 0))],
        out_shape=[
            jax.ShapeDtypeStruct((length, width), BF16),
            jax.ShapeDtypeStruct((HEADS, length, length // 2), BF16),
            jax.ShapeDtypeStruct((HEADS, 1, length), F32),
        ],
        scratch_shapes=[
            pltpu.VMEM((length, 2 * LANES + 2 * COORDS), BF16),
            pltpu.VMEM((2, 2 * LANES + 2 * COORDS, length), BF16),
            pltpu.VMEM((2, length // 2, length // 2), F32),
            pltpu.VMEM((2, COORDS, length), BF16),
        ],
        compiler_params=pltpu.CompilerParams(vmem_limit_bytes=58 * 1024 * 1024),
        cost_estimate=SMALL,
        name="attend",
    )(packed, bands, columns[0], seg[None], columns[1], columns[2], left[None], top[None])


def attend_back_kernel(first, qkv_ref, g_ref, probs_ref, inverse_ref, delta_ref, left_ref, top_ref, left_row, top_row, normed_ref,
                       bucket_ref, *rest):
    grad_ref, weight_ref, band_ref, key_across, marks, low_grads, spread, flip, normed_across, line_sums = rest[-10:]
    length = g_ref.shape[0]
    half = length // 2
    step = pl.program_id(0)

    @pl.when(step == 0)
    def _():
        normed_across[...] = normed_ref[...].T
        marks[:, :COORDS] = one_hot_lanes(left_ref[...], COORDS)
        marks[:, COORDS:] = one_hot_lanes(top_ref[...], COORDS)
        down = COORDS - 1 - lax.broadcasted_iota(jnp.int32, (COORDS, length), 0)
        left_marks = (down == left_row[...]).astype(F32).astype(BF16)
        top_marks = (down == top_row[...]).astype(F32).astype(BF16)
        for h in range(2):
            key_across[h, 64:64 + COORDS, :] = left_marks
            key_across[h, 64 + COORDS:, :] = top_marks
        turned = TILE - 1 - lax.broadcasted_iota(jnp.int32, (TILE, TILE), 0)
        flip[...] = (turned == lax.broadcasted_iota(jnp.int32, (TILE, TILE), 1)).astype(F32).astype(BF16)

    keys_t = qkv_ref[:, LANES:2 * LANES].T
    upper = lax.broadcasted_iota(jnp.int32, (length, LANES), 1) >= LANES // 2
    zero = jnp.zeros((), BF16)
    inverse = jnp.concatenate([inverse_ref[0], inverse_ref[1], jnp.zeros((6, length), F32)], axis=0).T
    grads_h, across_h, queries_h, delta_h = [], [], [], []
    for h in range(2):
        key_across[h, :64, :] = keys_t[h * 64:(h + 1) * 64]
        own = upper == (h == 1)
        mine = jnp.where(own, g_ref[...].astype(F32) * inverse[:, h:h + 1], 0.0).astype(BF16)
        grads_h.append(mine)
        across_h.append(mine.T)
        queries_h.append(jnp.where(own, qkv_ref[:, :LANES], zero))
        delta_h.append(delta_ref[pl.ds(2 * (first + step) + h, 1), :] * inverse_ref[h])
    values = qkv_ref[:, 2 * LANES:]

    def lanes(kind):
        return pl.ds(pl.multiple_of((step % 2) * 3 * LANES + kind * LANES, LANES), LANES)

    def spots(job):
        block, tile, h = job
        return (
            slice(block * half, (block + 1) * half),
            slice(block * half + tile * TILE, block * half + (tile + 1) * TILE),
            slice(tile * TILE, (tile + 1) * TILE),
        )

    def reach_of(job):
        rows, here, _ = spots(job)
        return dot(values[rows], across_h[job[2]][:, here])

    def push(job, reach):
        rows, here, across = spots(job)
        h = job[2]
        grads = (probs_ref[h, rows, across].astype(F32) * (reach - delta_h[h][:, here])).astype(BF16)
        low_grads[h, rows, across] = grads
        return dot(key_across[h, :, rows], grads)

    halves = {}

    def settle(job, both):
        block, tile, h = job
        rows, here, _ = spots(job)
        halves[job] = both[:64] * 0.125
        for t in range(2):
            spread[t, h * COORDS:(h + 1) * COORDS, here] = both[64 + t * COORDS:64 + (t + 1) * COORDS].astype(BF16)
        if h == 1:
            grad_ref[here, lanes(0)] = jnp.concatenate([halves[(block, tile, 0)], halves[job]], axis=0).T.astype(BF16)
        if h == 1 and tile == half // TILE - 1:
            grad_ref[rows, lanes(2)] = (
                dot(probs_ref[0, rows, :], grads_h[0][rows]) + dot(probs_ref[1, rows, :], grads_h[1][rows])
            ).astype(BF16)
            grad_ref[rows, lanes(1)] = (
                dot(low_grads[0, rows, :], queries_h[0][rows]) + dot(low_grads[1, rows, :], queries_h[1][rows])
            ).astype(BF16)

    jobs = [(block, tile, h) for block in range(2) for tile in range(half // TILE) for h in range(2)]
    reaching, pushed = [], []
    for job in jobs + [None] * 3:
        if job is not None:
            reaching.append((job, reach_of(job)))
        if reaching and (job is None or len(reaching) > 1):
            own, reach = reaching.pop(0)
            pushed.append((own, push(own, reach)))
        if pushed and (not reaching or len(pushed) > 1):
            settle(*pushed.pop(0))
    while reaching:
        own, reach = reaching.pop(0)
        pushed.append((own, push(own, reach)))
    while pushed:
        settle(*pushed.pop(0))

    @pl.when(step % 2 == 1)
    def _():
        weight_ref[...] = dot(normed_across[...], grad_ref[...]).astype(BF16)


    def part(h, block, down, tile):
        return low_grads[h, block * half + down * TILE:block * half + (down + 1) * TILE, tile * TILE:(tile + 1) * TILE].astype(F32)

    pressed = [dot(spread[t], marks[:, t * COORDS:(t + 1) * COORDS]) for t in range(2)]
    highs, rests = [], []
    for h in range(2):
        for square in (
            (part(h, 0, 0, 0) + part(h, 0, 1, 1)) + (part(h, 1, 0, 0) + part(h, 1, 1, 1)),
            part(h, 0, 1, 0) + part(h, 1, 1, 0),
            part(h, 0, 0, 1) + part(h, 1, 0, 1),
        ):
            high = square.astype(BF16)
            highs.append(high)
            rests.append((square - high.astype(F32)).astype(BF16))
    turned = dot(jnp.concatenate(highs + rests, axis=0), flip[...])
    for h in range(2):
        squares = [item[h * COORDS:(h + 1) * COORDS] for item in pressed]
        for place in range(3 * h, 3 * h + 3):
            squares.append(turned[place * TILE:(place + 1) * TILE] + turned[(place + 6) * TILE:(place + 7) * TILE])
        sums = [skew_sum(square) for square in squares]
        line_sums[pl.ds(pl.multiple_of((2 * step + h) * 8, 8), 8), :] = jnp.concatenate(
            sums + [jnp.zeros_like(sums[0])] * 3, axis=0
        )

    @pl.when(step == pl.num_programs(0) - 1)
    def _():
        lines = line_sums[...]
        count = lines.shape[0]
        high = lines.astype(BF16)
        both = dot(jnp.concatenate([high, (lines - high.astype(F32)).astype(BF16)], axis=0), bucket_ref[...])
        both = both[:count] + both[count:]
        for head in range(count // 8):
            picked = [both[head * 8 + t:head * 8 + t + 1, t * LANES:(t + 1) * LANES] for t in range(5)]
            band_ref[head] = jnp.concatenate(
                [picked[2] + picked[3] + picked[4], picked[0], picked[1], jnp.zeros((5, LANES), F32)], axis=0
            )


def attend_back(first, count, packed, grad_attended, probs, inverse, delta, left, top, columns, normed, buckets, *deps):
    length, width = grad_attended.shape
    column = pl.BlockSpec((length, 1), lambda g: (0, 0))
    row = pl.BlockSpec((1, length), lambda g: (0, 0))
    return pl.pallas_call(
        functools.partial(attend_back_kernel, first),
        grid=(count,),
        in_specs=[
            pl.BlockSpec((length, 3 * LANES), lambda g: (0, first + g)),
            pl.BlockSpec((length, LANES), lambda g: (0, first + g)),
            pl.BlockSpec((2, length, length // 2), lambda g: (first + g, 0, 0)),
            pl.BlockSpec((2, 1, length), lambda g: (first + g, 0, 0)),
            pl.BlockSpec(delta.shape, lambda g: (0, 0)),
            column, column, row, row,
            pl.BlockSpec((length, width), lambda g: (0, 0)),
            pl.BlockSpec(buckets.shape, lambda g: (0, 0)),
        ] + [pl.BlockSpec(memory_space=pl.ANY)] * len(deps),
        out_specs=[
            pl.BlockSpec((length, 6 * LANES), lambda g: (0, g // 2)),
            pl.BlockSpec((width, 6 * LANES), lambda g: (0, g // 2)),
            pl.BlockSpec((2 * count, 8, LANES), lambda g: (0, 0, 0)),
        ],
        out_shape=[
            jax.ShapeDtypeStruct((length, 3 * LANES * count), BF16),
            jax.ShapeDtypeStruct((width, 3 * LANES * count), BF16),
            jax.ShapeDtypeStruct((2 * count, 8, LANES), F32),
        ],
        scratch_shapes=[
            pltpu.VMEM((2, 64 + 2 * COORDS, length), BF16),
            pltpu.VMEM((length, 2 * COORDS), BF16),
            pltpu.VMEM((2, length, length // 2), BF16),
            pltpu.VMEM((2, 2 * COORDS, length), BF16),
            pltpu.VMEM((TILE, TILE), BF16),
            pltpu.VMEM((width, length), BF16),
            pltpu.VMEM((16 * count, 2 * TILE), F32),
        ],
        compiler_params=pltpu.CompilerParams(vmem_limit_bytes=58 * 1024 * 1024),
        cost_estimate=SMALL,
        name="attend_back",
    )(packed, grad_attended, probs, inverse, delta, columns[1], columns[2], left[None], top[None], normed, buckets, *deps)


ROOT = float(np.sqrt(2.0 / np.pi))


def feed_kernel(width, steps, kept, att_ref, start_ref, up_ref, inner_ref, outer_ref, output_ref, gain_ref,
                middle_ref, act_ref, back_ref, early_ref, late_ref, active, inner_back, normed, upstream):
    step = pl.program_id(0)
    parts = inner_ref.shape[1] // width

    @pl.when(step < steps)
    def _():
        size = att_ref.shape[0]
        rows = pl.ds(pl.multiple_of(step * size, size), size)
        up = up_ref[...]
        upstream[rows, :] = up
        middle = start_ref[...] + dot(att_ref[...], output_ref[...])
        middle_ref[...] = middle
        root = lax.rsqrt(jnp.mean(middle * middle, axis=1, keepdims=True) + 1e-06)
        low = (middle * root * gain_ref[...]).astype(BF16)
        normed[rows, :] = low

        def products(part):
            own = slice(part * width, (part + 1) * width)
            return dot(low, inner_ref[:, own]), dot(up, outer_ref[:, own], NT)

        def finish(part, point, reach):
            own = slice(part * width, (part + 1) * width)
            square = point * point
            bend = jnp.tanh(ROOT * point * (1.0 + 0.044715 * square))
            half = 0.5 + 0.5 * bend
            act = (point * half).astype(BF16)
            slope = half + (0.5 * ROOT) * point * (1.0 - bend * bend) * (1.0 + (3 * 0.044715) * square)
            grads = (slope * reach).astype(BF16)
            act_ref[:, own] = act
            back_ref[:, own] = grads
            active[rows, own] = act
            inner_back[rows, own] = grads

        held = products(0)
        for part in range(1, parts):
            following = products(part)
            finish(part - 1, *held)
            held = following
        finish(parts - 1, *held)

    @pl.when(jnp.logical_and(step >= steps, step < steps + parts))
    def _():
        own = pl.ds(pl.multiple_of((step - steps) * width, width), width)
        early_ref[...] = dot(active[:, own], upstream[...], TN).astype(BF16)

    def inner_grad():
        own = pl.ds(pl.multiple_of((step - steps - parts) * width, width), width)
        return dot(normed[...], inner_back[:, own], TN).astype(BF16)

    @pl.when(jnp.logical_and(step >= steps + parts, step < steps + parts + kept))
    def _():
        early_ref[...] = inner_grad()

    @pl.when(step >= steps + parts + kept)
    def _():
        late_ref[...] = inner_grad()


def weight_specs(width, parts, places):
    once = pl.Buffered(1)
    specs = [
        pl.BlockSpec((width, parts * width), lambda g: (0, 0), pipeline_mode=once),
        pl.BlockSpec((width, parts * width), lambda g: (0, 1), pipeline_mode=once),
        pl.BlockSpec((width, width), lambda g: (0, 2 * parts), pipeline_mode=once),
        pl.BlockSpec((1, width), lambda g: (0, 0)),
    ]
    return [specs[place] for place in places]


def feed(kept, attended, start, upstream, weights, gain):
    length, width = attended.shape
    steps = length // TILE
    parts = weights.shape[1] // width // 2
    rows = lambda g: (jnp.minimum(g, steps - 1), 0)
    tile = pl.BlockSpec((TILE, width), rows)
    broad = pl.BlockSpec((TILE, parts * width), rows)
    return pl.pallas_call(
        functools.partial(feed_kernel, width, steps, kept),
        grid=(steps + 2 * parts,),
        in_specs=[tile, tile, tile] + weight_specs(width, parts, (0, 1, 2, 3)),
        out_specs=[
            tile, broad, broad,
            pl.BlockSpec((width, width), lambda g: (0, jnp.clip(g - steps, 0, parts + kept - 1))),
            pl.BlockSpec((width, width), lambda g: (0, jnp.maximum(g - steps - parts - kept, 0))),
        ],
        out_shape=[
            jax.ShapeDtypeStruct((length, width), F32),
            jax.ShapeDtypeStruct((length, parts * width), BF16),
            jax.ShapeDtypeStruct((length, parts * width), BF16),
            jax.ShapeDtypeStruct((width, (parts + kept) * width), BF16),
            jax.ShapeDtypeStruct((width, (parts - kept) * width), BF16),
        ],
        scratch_shapes=[pltpu.VMEM((length, parts * width), BF16)] * 2 + [pltpu.VMEM((length, width), BF16)] * 2,
        compiler_params=pltpu.CompilerParams(vmem_limit_bytes=58 * 1024 * 1024),
        cost_estimate=SMALL,
        name="feed",
    )(attended, start, upstream, weights, weights, weights, gain)


def feed_back_kernel(width, steps, att_ref, middle_ref, up_ref, act_ref, back_ref, inner_ref, outer_ref, output_ref, gain_ref,
                     *rest):
    layer_ref, out_ref, seen_ref, delta_ref, weight_ref, low_middle, attended = rest[-7:]
    step = pl.program_id(0)

    @pl.when(step < steps)
    def _():
        size = att_ref.shape[0]
        rows = pl.ds(pl.multiple_of(step * size, size), size)
        att = att_ref[...]
        attended[rows, :] = att
        gain = gain_ref[...]
        middle = middle_ref[...]
        back = dot(back_ref[...], inner_ref[...], NT)
        result = middle
        for part in range(act_ref.shape[1] // width):
            own = slice(part * width, (part + 1) * width)
            result = result + dot(act_ref[:, own], outer_ref[:, own])
        root = lax.rsqrt(jnp.mean(middle * middle, axis=1, keepdims=True) + 1e-06)
        scaled = middle * root
        slant = jnp.mean(back * scaled * gain, axis=1, keepdims=True)
        grad_middle = up_ref[...].astype(F32) + root * (gain * back - scaled * slant)
        out_ref[...] = grad_middle
        rounded = grad_middle.astype(BF16)
        low_middle[rows, :] = rounded
        layer_ref[...] = result.astype(BF16)
        seen = dot(rounded, output_ref[...], NT).astype(BF16)
        seen_ref[...] = seen
        product = att.astype(F32) * seen.astype(F32)
        high = product.astype(BF16)
        low = (product - high.astype(F32)).astype(BF16)
        head = lax.broadcasted_iota(jnp.int32, (16, width), 0)
        lane = lax.broadcasted_iota(jnp.int32, (16, width), 1)
        marks = jnp.logical_and(lane >= head * 64, lane < head * 64 + 64).astype(F32).astype(BF16)
        delta_ref[...] = dot(marks, high, NT) + dot(marks, low, NT)

    @pl.when(step == steps)
    def _():
        weight_ref[...] = dot(attended[...], low_middle[...], TN).astype(BF16)


def feed_back(attended, middle, upstream, act, back, weights, gain, *deps):
    length, width = attended.shape
    steps = length // TILE
    parts = weights.shape[1] // width // 2
    rows = lambda g: (jnp.minimum(g, steps - 1), 0)
    tile = pl.BlockSpec((TILE, width), rows)
    broad = pl.BlockSpec((TILE, parts * width), rows)
    tokens = jax.ShapeDtypeStruct((length, width), BF16)
    return pl.pallas_call(
        functools.partial(feed_back_kernel, width, steps),
        grid=(steps + 1,),
        in_specs=[tile, tile, tile, broad, broad] + weight_specs(width, parts, (0, 1, 2, 3))
        + [pl.BlockSpec(memory_space=pl.ANY)] * len(deps),
        out_specs=[
            tile, tile, tile,
            pl.BlockSpec((16, TILE), lambda g: (0, jnp.minimum(g, steps - 1))),
            pl.BlockSpec((width, width), lambda g: (0, 0)),
        ],
        out_shape=[
            tokens,
            jax.ShapeDtypeStruct((length, width), F32),
            tokens,
            jax.ShapeDtypeStruct((16, length), F32),
            jax.ShapeDtypeStruct((width, width), BF16),
        ],
        scratch_shapes=[pltpu.VMEM((length, width), BF16)] * 2,
        compiler_params=pltpu.CompilerParams(vmem_limit_bytes=58 * 1024 * 1024),
        cost_estimate=SMALL,
        name="feed_back",
    )(attended, middle, upstream, act, back, weights, weights, weights, gain, *deps)


def last_kernel(start_ref, middle_ref, gain_ref, weight_ref, *rest):
    grads_refs, out_ref = rest[:1], rest[-1]
    start = start_ref[...]
    gain = gain_ref[...]
    root = lax.rsqrt(jnp.mean(start * start, axis=1, keepdims=True) + 1e-06)
    scaled = start * root
    low = 0
    back = 0.0
    for grads_ref in grads_refs:
        high = low + grads_ref.shape[1]
        back = back + dot(grads_ref[...], weight_ref[:, low:high], NT)
        low = high
    slant = jnp.mean(back * scaled * gain, axis=1, keepdims=True)
    out_ref[...] = middle_ref[...] + root * (gain * back - scaled * slant)


def last(start, middle, gain, weights, grads, *deps):
    length, width = start.shape
    tile = pl.BlockSpec((TILE, width), lambda g: (g, 0))
    total = sum(item.shape[1] for item in grads)
    return pl.pallas_call(
        last_kernel,
        grid=(length // TILE,),
        in_specs=[
            tile, tile, pl.BlockSpec((1, width), lambda g: (0, 0)),
            pl.BlockSpec((width, total), lambda g: (0, 0), pipeline_mode=pl.Buffered(1)),
        ]
        + [pl.BlockSpec((TILE, item.shape[1]), lambda g: (g, 0)) for item in grads]
        + [pl.BlockSpec(memory_space=pl.ANY)] * len(deps),
        out_specs=tile,
        out_shape=jax.ShapeDtypeStruct((length, width), F32),
        compiler_params=pltpu.CompilerParams(vmem_limit_bytes=24 * 1024 * 1024),
        cost_estimate=SMALL,
        name="last",
    )(start, middle, gain, weights, *grads, *deps)


def half_kernel(count, core_ref, *refs):
    out_ref = refs[-1]
    low = 0
    for array_ref in refs[:count]:
        high = low + array_ref.shape[-1]
        for place in range(array_ref.shape[0]):
            out_ref[0, place, :, low:high] = array_ref[place, 0, 0]
        low = high


def merge_kernel(count, core_ref, *refs):
    came_ref, out_ref = refs[count], refs[-1]
    low = 0
    for array_ref in refs[:count]:
        high = low + array_ref.shape[-1]
        for place in range(array_ref.shape[0]):
            out_ref[0, place, :, low:high] = (
                array_ref[place, 0, 0].astype(F32) + came_ref[0, place, :, low:high].astype(F32)
            ).astype(BF16)
        low = high


def core_part(kernel, core, arrays, owned, came, *deps):
    outer = arrays[0].shape[0] // owned // 8
    width = sum(array.shape[1] for array in arrays)
    block = pl.BlockSpec((1, outer, owned, width), lambda g, core: (g, 0, 0, 0))
    return pl.pallas_call(
        functools.partial(kernel, len(arrays)),
        grid_spec=pltpu.PrefetchScalarGridSpec(
            num_scalar_prefetch=1,
            grid=(4,),
            in_specs=[
                pl.BlockSpec((outer, 1, 1, owned, array.shape[1]), lambda g, core: (0, g, core[0], 0, 0)) for array in arrays
            ]
            + [block] * len(came) + [pl.BlockSpec(memory_space=pl.ANY)] * len(deps),
            out_specs=block,
        ),
        out_shape=jax.ShapeDtypeStruct((4, outer, owned, width), BF16),
        compiler_params=pltpu.CompilerParams(vmem_limit_bytes=20 * 1024 * 1024),
        cost_estimate=SMALL,
        name="core_part",
    )(core, *[array.reshape(outer, 4, 2, owned, array.shape[1]) for array in arrays], *came, *deps)


def gate_kernel(*refs):
    pass


def gate(array, *deps):
    return pl.pallas_call(
        gate_kernel,
        in_specs=[pl.BlockSpec(memory_space=pl.ANY)] * (1 + len(deps)),
        out_specs=pl.BlockSpec(memory_space=pl.ANY),
        out_shape=jax.ShapeDtypeStruct(array.shape, array.dtype),
        input_output_aliases={0: 0},
        cost_estimate=SMALL,
        name="gate",
    )(array, *deps)


def gather_sum_kernel(array_ref, *rest):
    out_ref = rest[-1]
    total = array_ref[0].astype(F32)
    for place in range(1, array_ref.shape[0]):
        total = total + array_ref[place].astype(F32)
    out_ref[...] = total.astype(out_ref.dtype)


def gather_sum(array, *deps):
    inner, outer, owned, width = array.shape
    return pl.pallas_call(
        gather_sum_kernel,
        grid=(outer,),
        in_specs=[pl.BlockSpec((inner, 1, owned, width), lambda g: (0, g, 0, 0))] + [pl.BlockSpec(memory_space=pl.ANY)] * len(deps),
        out_specs=pl.BlockSpec((1, owned, width), lambda g: (g, 0, 0)),
        out_shape=jax.ShapeDtypeStruct((outer, owned, width), BF16),
        compiler_params=pltpu.CompilerParams(vmem_limit_bytes=20 * 1024 * 1024),
        cost_estimate=SMALL,
        name="gather_sum",
    )(array, *deps)


def finish_kernel(width, level_ref, trio_ref, gain_ref, *out_refs):
    total = level_ref[0].astype(F32)
    for place in range(1, level_ref.shape[0]):
        total = total + level_ref[place].astype(F32)
    out_refs[0][...] = total[:, :width]
    for pair in range(width // LANES):
        for kind in range(3):
            low = width + (3 * pair + kind) * LANES
            out_refs[1 + kind][:, pair * LANES:(pair + 1) * LANES] = total[:, low:low + LANES]
    own = jnp.sum(trio_ref[...].astype(F32) * total[:, width:4 * width], axis=1, keepdims=True)
    out_refs[4][...] = jnp.broadcast_to(own / gain_ref[...].astype(F32), out_refs[4].shape)
    out_refs[5][...] = total[:, 4 * width:]


def finish(level, trio, gain):
    owned, width = trio.shape[0], trio.shape[1] // 3
    square = jax.ShapeDtypeStruct((owned, width), F32)
    return pl.pallas_call(
        functools.partial(finish_kernel, width),
        out_shape=[square] * 4 + [
            jax.ShapeDtypeStruct((owned, LANES), F32),
            jax.ShapeDtypeStruct((owned, level.shape[2] - 4 * width), F32),
        ],
        compiler_params=pltpu.CompilerParams(vmem_limit_bytes=20 * 1024 * 1024),
        cost_estimate=SMALL,
        name="finish",
    )(level, trio, gain)


def weave_kernel(core_ref, own_ref, came_ref, out_ref):
    core = core_ref[0]
    for place in range(own_ref.shape[0]):
        out_ref[0, place, core] = own_ref[place, 0]
        out_ref[0, place, 1 - core] = came_ref[place, 0]


def weave(core, own, came, width):
    inner, outer, owned = own.shape[:3]
    block = pl.BlockSpec((inner, 1, owned, width), lambda g, core: (0, g, 0, 0))
    return pl.pallas_call(
        weave_kernel,
        grid_spec=pltpu.PrefetchScalarGridSpec(
            num_scalar_prefetch=1,
            grid=(outer,),
            in_specs=[block, block],
            out_specs=pl.BlockSpec((1, inner, 2, owned, width), lambda g, core: (g, 0, 0, 0, 0)),
        ),
        out_shape=jax.ShapeDtypeStruct((outer, inner, 2, owned, width), BF16),
        compiler_params=pltpu.CompilerParams(vmem_limit_bytes=20 * 1024 * 1024),
        cost_estimate=SMALL,
        name="weave",
    )(core, own, came)


def turn(array, shift):
    return lax.dynamic_slice_in_dim(jnp.concatenate([array, array], axis=0), shift, array.shape[0], axis=0)


def long_start(segments):
    names = jnp.arange(8, dtype=jnp.int32)
    counts = jnp.sum((segments[None, :] == names[:, None]).astype(jnp.int32), axis=1)
    return jnp.sum((segments < jnp.argmax(counts).astype(jnp.int32)).astype(jnp.int32))


def member_groups(members, low, high):
    apart = 1 << low
    span = 1 << high
    return [
        [base + apart * place for place in range(span // apart)]
        for base in range(members)
        if (base & (span - 1) & ~(apart - 1)) == 0
    ]


def swap_cores(members, array):
    return lax.ppermute(array, "dp", [(place, place ^ 1) for place in range(members)])


def across_plane(members, array):
    return lax.all_to_all(array, "dp", 0, 0, axis_index_groups=member_groups(members, 1, 3))


def along_line(members, array):
    return lax.all_to_all(
        array, "dp", 0, 0, axis_index_groups=member_groups(members, 3, members.bit_length() - 1)
    )


def spread_line(members, array):
    outer = members // 8
    return lax.all_to_all(
        jnp.broadcast_to(array[None], (outer,) + array.shape), "dp", 0, 0,
        axis_index_groups=member_groups(members, 3, members.bit_length() - 1),
    )


def spread_plane(members, array):
    return across_plane(members, jnp.broadcast_to(array[None], (4,) + array.shape))


def per_device(
    members,
    tokens,
    image_features,
    segment_ids,
    box_left,
    box_top,
    cotangent,
    query_weight,
    key_weight,
    value_weight,
    output_weight,
    inner_weight,
    outer_weight,
    attention_gain,
    feed_gain,
    bias_tables,
):
    length, width = tokens.shape[1:]
    owned = query_weight.shape[0]
    parts = inner_weight.shape[1] // width
    spots = bias_tables.shape[0]

    small = jnp.concatenate(
        [
            attention_gain[:, None],
            feed_gain[:, None],
            jnp.pad(bias_tables, (0, 2 * owned - spots)).reshape(owned, 2),
            jnp.zeros((owned, LANES - 4), BF16),
        ],
        axis=1,
    )
    pairs = width // LANES
    trio = jnp.concatenate([query_weight, key_weight, value_weight], axis=1)
    trio = trio.reshape(owned, 3, pairs, LANES).transpose(0, 2, 1, 3).reshape(owned, 3 * width)
    core = (lax.axis_index("dp") & 1).reshape(1)
    inner_own = inner_weight.reshape(owned, width, parts).transpose(0, 2, 1).reshape(owned, parts * width)
    second = lax.all_gather(
        jnp.concatenate([inner_own, outer_weight.reshape(owned, parts * width), output_weight], axis=1),
        "dp", axis=0, tiled=True,
    )
    shift = long_start(segment_ids[0])
    segments, left, top = (turn(item[0], shift) for item in (segment_ids, box_left, box_top))
    start = turn(tokens[0], shift).astype(F32) + turn(image_features[0], shift).astype(F32)
    upstream = turn(cotangent[0], shift)
    root = lax.rsqrt(jnp.mean(start * start, axis=1, keepdims=True) + 1e-06)
    level = spread_line(members, jnp.concatenate([trio, small], axis=1))
    part = spread_plane(members, gate(level[:, :, 3 * width:], start))
    level = spread_plane(members, level[:, :, :3 * width])
    little = weave(core, part, swap_cores(members, part), LANES).reshape(width, LANES)
    gain_one = little[:, 0].astype(F32)[None]
    gain_two = little[:, 1].astype(F32)[None]
    bands = rows_of(little[:, 2:4].reshape(-1, 2 * owned)[:, :spots].reshape(3 * BUCKETS, HEADS))
    normed = (start * root * gain_one).astype(BF16)
    columns = [segments[:, None], left[:, None], top[:, None]]
    level = gate(level, upstream, normed, gain_two, bands, *columns)
    project = weave(core, level, swap_cores(members, level), 3 * width).reshape(width, 3 * width)
    scale = jnp.where(jnp.arange(3 * width) % (3 * LANES) < LANES, 0.125, 1.0)[None]
    packed = (dot(normed, project) * scale).astype(BF16)
    attended, probs, inverse = attend(packed, bands, segments, left, top, columns)

    kept = parts // 2
    middle, act, inner_back, early, late = feed(kept, attended, start, upstream, second, gain_two)
    early_sum = lax.psum_scatter(early, "dp", scatter_dimension=0, tiled=True)
    sent = core_part(half_kernel, 1 - core, [late], owned, [])
    late_one = core_part(merge_kernel, core, [late], owned, [swap_cores(members, sent)])
    late_two = across_plane(members, late_one)

    layer, grad_middle, grad_attended, delta, output_grad = feed_back(
        attended, middle, upstream, act, inner_back, second, gain_two, late_one
    )
    late_two = gather_sum(late_two, delta)
    late_last = jnp.sum(along_line(members, late_two).astype(F32), axis=0)

    grads, weights, bands_grad = attend_back(
        0, pairs, packed, grad_attended, probs, inverse, delta, left, top, columns, normed, bucket_marks(), late_two
    )
    tables_grad = bands_grad[:, :3, :BUCKETS].transpose(1, 2, 0).reshape(-1)
    room = -(-tables_grad.size // owned // LANES) * LANES
    tables_grad = jnp.pad(tables_grad, (0, owned * room - tables_grad.size)).astype(BF16).reshape(1, owned, room)
    tables_grad = jnp.broadcast_to(tables_grad, (members, owned, room)).reshape(width, room)
    group = [output_grad, weights, tables_grad]
    sent = core_part(half_kernel, 1 - core, group, owned, [], late_last)
    trio_one = core_part(merge_kernel, core, group, owned, [swap_cores(members, sent)])
    trio_two = across_plane(members, trio_one)

    input_gradient = turn(last(start, grad_middle, gain_one, project, [grads], trio_one), length - shift)[None]
    layer = turn(gate(layer, trio_one), length - shift)[None]

    trio_two = gather_sum(trio_two, input_gradient, layer)
    outer_sum = early_sum[:, :parts * width].astype(F32).reshape(outer_weight.shape)
    inner_sum = jnp.concatenate([early_sum[:, parts * width:].astype(F32), late_last], axis=1)
    inner_sum = inner_sum.reshape(owned, parts, width).transpose(0, 2, 1).reshape(owned, parts * width)
    feed_gain_grad = jnp.sum(inner_weight.astype(F32) * inner_sum, axis=1) / feed_gain.astype(F32)
    output_sum, query_sum, key_sum, value_sum, gain_grad, tables_last = finish(
        gate(along_line(members, trio_two), inner_sum, outer_sum), trio, attention_gain[:, None]
    )
    tables_last = lax.dynamic_slice_in_dim(tables_last.reshape(-1), lax.axis_index("dp") * spots, spots)
    return (
        layer,
        input_gradient,
        query_sum,
        key_sum,
        value_sum,
        output_sum,
        inner_sum,
        outer_sum,
        gain_grad[:, 0],
        feed_gain_grad,
        tables_last,
    )


def solution(mesh):
    rows = P("dp", None)
    cubes = P("dp", None, None)
    line = P("dp")
    return jax.shard_map(
        functools.partial(per_device, mesh.shape["dp"]),
        mesh=mesh,
        in_specs=(cubes, cubes, rows, rows, rows, cubes) + (rows,) * 6 + (line,) * 3,
        out_specs=(cubes, cubes) + (rows,) * 6 + (line,) * 3,
        check_vma=False,
    )
```

```python
import functools

import numpy as np
import jax
import jax.numpy as jnp
from jax import lax
from jax.sharding import PartitionSpec as P
from jax.experimental import pallas as pl
from jax.experimental.pallas import tpu as pltpu

HEADS = 12
BUCKETS = 32
thresholds = (1, 2, 3, 4, 5, 6, 7, 8, 11, 16, 22, 32, 45, 64, 90)
COORDS = 256
TILE = 256
LANES = 128
AHEAD = 3
SMALL = pl.CostEstimate(flops=10**8, bytes_accessed=10**5, transcendentals=0)
F32 = jnp.float32
BF16 = jnp.bfloat16
NT = (((1,), (1,)), ((), ()))
NN = (((1,), (0,)), ((), ()))
TN = (((0,), (0,)), ((), ()))


def bucket_of(offset):
    magnitude = np.zeros(offset.shape, np.int32)
    for limit in thresholds:
        magnitude = magnitude + (np.abs(offset) >= limit).astype(np.int32)
    return magnitude + BUCKETS // 2 * (offset > 0).astype(np.int32)


def dot(left, right, dims=NN):
    return lax.dot_general(left, right, dims, preferred_element_type=F32)


def rows_of(tables):
    spot = np.arange(2 * TILE)
    signed = np.where(spot < TILE, spot, spot - 2 * TILE)
    marks = np.zeros((3, BUCKETS, 8, 2 * TILE), np.float32)
    picks = ((1, -signed), (2, -signed), (0, -signed), (0, TILE - signed), (0, -TILE - signed))
    for place, (table_index, offset) in enumerate(picks):
        marks[table_index, bucket_of(offset), place, spot] = 1.0
    marks = marks.reshape(3 * BUCKETS, 16 * TILE).astype(BF16)
    return dot(tables, jnp.asarray(marks), TN).reshape(HEADS, 8, 2 * TILE)


def bucket_marks():
    spot = np.arange(2 * TILE)
    falling = TILE - 1 - spot
    rising = spot - (TILE - 1)
    offsets = np.stack([falling, falling, rising, TILE + rising, rising - TILE], axis=1)
    marks = bucket_of(offsets)[:, :, None] == np.arange(LANES)
    return jnp.asarray(marks.astype(BF16).reshape(2 * TILE, 5 * LANES))


def toeplitz(row):
    wide = jnp.broadcast_to(row, (TILE, 2 * TILE))
    return pltpu.roll(wide, 0, axis=1, stride=1, stride_axis=0)[:, :TILE]


def skew_sum(square):
    wide = jnp.concatenate([square, jnp.zeros_like(square)], axis=1)
    return jnp.sum(pltpu.roll(wide, 0, axis=1, stride=1, stride_axis=0), axis=0, keepdims=True)


def one_hot_lanes(column, width):
    return (column == lax.broadcasted_iota(jnp.int32, (column.shape[0], width), 1)).astype(F32).astype(BF16)


def attend_kernel(qkv_ref, band_ref, seg_ref, seg_row, left_ref, top_ref, left_row, top_row, out_ref, probs_ref, sums_ref,
                key_side, query_side, position, marks):
    length = qkv_ref.shape[0]
    half = length // 2

    @pl.when(pl.program_id(0) == 0)
    def _():
        key_side[:, LANES:2 * LANES] = one_hot_lanes(seg_ref[...], LANES)
        key_side[:, 2 * LANES:2 * LANES + COORDS] = one_hot_lanes(left_ref[...], COORDS)
        key_side[:, 2 * LANES + COORDS:] = one_hot_lanes(top_ref[...], COORDS)
        down = lax.broadcasted_iota(jnp.int32, (LANES, length), 0)
        other = jnp.where(jnp.logical_and(down < 8, down != seg_row[...]), F32(-1e30), F32(0)).astype(BF16)
        query_side[0, LANES:2 * LANES, :] = other
        query_side[1, LANES:2 * LANES, :] = other
        down = lax.broadcasted_iota(jnp.int32, (COORDS, length), 0)
        marks[0] = (down == left_row[...]).astype(F32).astype(BF16)
        marks[1] = (down == top_row[...]).astype(F32).astype(BF16)
        query_side[0, 64:LANES, :] = jnp.zeros((64, length), BF16)
        query_side[1, :64, :] = jnp.zeros((64, length), BF16)

    key_side[:, :LANES] = qkv_ref[:, LANES:2 * LANES]
    values_across = qkv_ref[:, 2 * LANES:].T
    queries_across = qkv_ref[:, :LANES].T
    for h in range(2):
        bands = band_ref[h]
        own = slice(h * 64, (h + 1) * 64)
        query_side[h, own, :] = queries_across[own]
        middle, below, above = (toeplitz(bands[t:t + 1]) for t in (2, 3, 4))
        position[h, :TILE, :TILE] = middle
        position[h, TILE:, TILE:] = middle
        position[h, TILE:, :TILE] = below
        position[h, :TILE, TILE:] = above

    for t in range(2):
        low = 2 * LANES + t * COORDS
        grids = jnp.concatenate([toeplitz(band_ref[h, t:t + 1]) for h in range(2)], axis=0).astype(BF16)
        spread = dot(grids, marks[t]).astype(BF16)
        for h in range(2):
            query_side[h, low:low + COORDS, :] = spread[h * COORDS:(h + 1) * COORDS]

    def logits_of(block, tile, h):
        rows = slice(block * half, (block + 1) * half)
        here = slice(block * half + tile * TILE, block * half + (tile + 1) * TILE)
        return dot(key_side[rows, :], query_side[h, :, here]) + position[h, :, tile * TILE:(tile + 1) * TILE]

    def finish(block, tile, h, logits):
        rows = slice(block * half, (block + 1) * half)
        across = slice(tile * TILE, (tile + 1) * TILE)
        here = slice(block * half + tile * TILE, block * half + (tile + 1) * TILE)
        raised = jnp.exp(logits - jnp.max(logits, axis=0, keepdims=True))
        inverse = 1.0 / jnp.sum(raised, axis=0, keepdims=True)
        low = raised.astype(BF16)
        probs_ref[h, rows, across] = low
        sums_ref[h, :, here] = inverse
        return dot(values_across[h * 64:(h + 1) * 64, rows], low) * inverse

    jobs = [(block, tile, h) for block in range(2) for tile in range(half // TILE) for h in range(2)]
    pieces = {}

    def close(job, logits):
        block, tile, h = job
        pieces[job] = finish(*job, logits)
        if h == 1:
            here = slice(block * half + tile * TILE, block * half + (tile + 1) * TILE)
            out_ref[here, :] = jnp.concatenate([pieces[(block, tile, 0)], pieces[(block, tile, 1)]], axis=0).T.astype(BF16)

    waiting = []
    for job in jobs:
        waiting.append((job, logits_of(*job)))
        if len(waiting) > AHEAD:
            close(*waiting.pop(0))
    for item in waiting:
        close(*item)


def attend(packed, bands, seg, left, top, columns):
    length, width = packed.shape[0], packed.shape[1] // 3
    pair = pl.BlockSpec((length, LANES), lambda g: (0, g))
    column = pl.BlockSpec((length, 1), lambda g: (0, 0))
    row = pl.BlockSpec((1, length), lambda g: (0, 0))
    return pl.pallas_call(
        attend_kernel,
        grid=(HEADS // 2,),
        in_specs=[
            pl.BlockSpec((length, 3 * LANES), lambda g: (0, g)),
            pl.BlockSpec((2, 8, 2 * TILE), lambda g: (g, 0, 0)),
            column, row, column, column, row, row,
        ],
        out_specs=[pair, pl.BlockSpec((2, length, length // 2), lambda g: (g, 0, 0)), pl.BlockSpec((2, 1, length), lambda g: (g, 0, 0))],
        out_shape=[
            jax.ShapeDtypeStruct((length, width), BF16),
            jax.ShapeDtypeStruct((HEADS, length, length // 2), BF16),
            jax.ShapeDtypeStruct((HEADS, 1, length), F32),
        ],
        scratch_shapes=[
            pltpu.VMEM((length, 2 * LANES + 2 * COORDS), BF16),
            pltpu.VMEM((2, 2 * LANES + 2 * COORDS, length), BF16),
            pltpu.VMEM((2, length // 2, length // 2), F32),
            pltpu.VMEM((2, COORDS, length), BF16),
        ],
        compiler_params=pltpu.CompilerParams(vmem_limit_bytes=58 * 1024 * 1024),
        cost_estimate=SMALL,
        name="attend",
    )(packed, bands, columns[0], seg[None], columns[1], columns[2], left[None], top[None])


def attend_back_kernel(first, qkv_ref, g_ref, probs_ref, inverse_ref, delta_ref, left_ref, top_ref, left_row, top_row, normed_ref,
                       bucket_ref, *rest):
    grad_ref, weight_ref, band_ref, key_across, marks, low_grads, spread, flip, normed_across, line_sums = rest[-10:]
    length = g_ref.shape[0]
    half = length // 2
    step = pl.program_id(0)

    @pl.when(step == 0)
    def _():
        normed_across[...] = normed_ref[...].T
        marks[:, :COORDS] = one_hot_lanes(left_ref[...], COORDS)
        marks[:, COORDS:] = one_hot_lanes(top_ref[...], COORDS)
        down = COORDS - 1 - lax.broadcasted_iota(jnp.int32, (COORDS, length), 0)
        left_marks = (down == left_row[...]).astype(F32).astype(BF16)
        top_marks = (down == top_row[...]).astype(F32).astype(BF16)
        for h in range(2):
            key_across[h, 64:64 + COORDS, :] = left_marks
            key_across[h, 64 + COORDS:, :] = top_marks
        turned = TILE - 1 - lax.broadcasted_iota(jnp.int32, (TILE, TILE), 0)
        flip[...] = (turned == lax.broadcasted_iota(jnp.int32, (TILE, TILE), 1)).astype(F32).astype(BF16)

    keys_t = qkv_ref[:, LANES:2 * LANES].T
    upper = lax.broadcasted_iota(jnp.int32, (length, LANES), 1) >= LANES // 2
    zero = jnp.zeros((), BF16)
    inverse = jnp.concatenate([inverse_ref[0], inverse_ref[1], jnp.zeros((6, length), F32)], axis=0).T
    grads_h, across_h, queries_h, delta_h = [], [], [], []
    for h in range(2):
        key_across[h, :64, :] = keys_t[h * 64:(h + 1) * 64]
        own = upper == (h == 1)
        mine = jnp.where(own, g_ref[...].astype(F32) * inverse[:, h:h + 1], 0.0).astype(BF16)
        grads_h.append(mine)
        across_h.append(mine.T)
        queries_h.append(jnp.where(own, qkv_ref[:, :LANES], zero))
        delta_h.append(delta_ref[pl.ds(2 * (first + step) + h, 1), :] * inverse_ref[h])
    values = qkv_ref[:, 2 * LANES:]

    def lanes(kind):
        return pl.ds(pl.multiple_of((step % 2) * 3 * LANES + kind * LANES, LANES), LANES)

    def spots(job):
        block, tile, h = job
        return (
            slice(block * half, (block + 1) * half),
            slice(block * half + tile * TILE, block * half + (tile + 1) * TILE),
            slice(tile * TILE, (tile + 1) * TILE),
        )

    def reach_of(job):
        rows, here, _ = spots(job)
        return dot(values[rows], across_h[job[2]][:, here])

    def push(job, reach):
        rows, here, across = spots(job)
        h = job[2]
        grads = (probs_ref[h, rows, across].astype(F32) * (reach - delta_h[h][:, here])).astype(BF16)
        low_grads[h, rows, across] = grads
        return dot(key_across[h, :, rows], grads)

    halves = {}

    def settle(job, both):
        block, tile, h = job
        rows, here, _ = spots(job)
        halves[job] = both[:64] * 0.125
        for t in range(2):
            spread[t, h * COORDS:(h + 1) * COORDS, here] = both[64 + t * COORDS:64 + (t + 1) * COORDS].astype(BF16)
        if h == 1:
            grad_ref[here, lanes(0)] = jnp.concatenate([halves[(block, tile, 0)], halves[job]], axis=0).T.astype(BF16)
        if h == 1 and tile == half // TILE - 1:
            grad_ref[rows, lanes(2)] = (
                dot(probs_ref[0, rows, :], grads_h[0][rows]) + dot(probs_ref[1, rows, :], grads_h[1][rows])
            ).astype(BF16)
            grad_ref[rows, lanes(1)] = (
                dot(low_grads[0, rows, :], queries_h[0][rows]) + dot(low_grads[1, rows, :], queries_h[1][rows])
            ).astype(BF16)

    jobs = [(block, tile, h) for block in range(2) for tile in range(half // TILE) for h in range(2)]
    reaching, pushed = [], []
    for job in jobs + [None] * 3:
        if job is not None:
            reaching.append((job, reach_of(job)))
        if reaching and (job is None or len(reaching) > 1):
            own, reach = reaching.pop(0)
            pushed.append((own, push(own, reach)))
        if pushed and (not reaching or len(pushed) > 1):
            settle(*pushed.pop(0))
    while reaching:
        own, reach = reaching.pop(0)
        pushed.append((own, push(own, reach)))
    while pushed:
        settle(*pushed.pop(0))

    @pl.when(step % 2 == 1)
    def _():
        weight_ref[...] = dot(normed_across[...], grad_ref[...]).astype(BF16)


    def part(h, block, down, tile):
        return low_grads[h, block * half + down * TILE:block * half + (down + 1) * TILE, tile * TILE:(tile + 1) * TILE].astype(F32)

    pressed = [dot(spread[t], marks[:, t * COORDS:(t + 1) * COORDS]) for t in range(2)]
    highs, rests = [], []
    for h in range(2):
        for square in (
            (part(h, 0, 0, 0) + part(h, 0, 1, 1)) + (part(h, 1, 0, 0) + part(h, 1, 1, 1)),
            part(h, 0, 1, 0) + part(h, 1, 1, 0),
            part(h, 0, 0, 1) + part(h, 1, 0, 1),
        ):
            high = square.astype(BF16)
            highs.append(high)
            rests.append((square - high.astype(F32)).astype(BF16))
    turned = dot(jnp.concatenate(highs + rests, axis=0), flip[...])
    for h in range(2):
        squares = [item[h * COORDS:(h + 1) * COORDS] for item in pressed]
        for place in range(3 * h, 3 * h + 3):
            squares.append(turned[place * TILE:(place + 1) * TILE] + turned[(place + 6) * TILE:(place + 7) * TILE])
        sums = [skew_sum(square) for square in squares]
        line_sums[pl.ds(pl.multiple_of((2 * step + h) * 8, 8), 8), :] = jnp.concatenate(
            sums + [jnp.zeros_like(sums[0])] * 3, axis=0
        )

    @pl.when(step == pl.num_programs(0) - 1)
    def _():
        lines = line_sums[...]
        count = lines.shape[0]
        high = lines.astype(BF16)
        both = dot(jnp.concatenate([high, (lines - high.astype(F32)).astype(BF16)], axis=0), bucket_ref[...])
        both = both[:count] + both[count:]
        for head in range(count // 8):
            picked = [both[head * 8 + t:head * 8 + t + 1, t * LANES:(t + 1) * LANES] for t in range(5)]
            band_ref[head] = jnp.concatenate(
                [picked[2] + picked[3] + picked[4], picked[0], picked[1], jnp.zeros((5, LANES), F32)], axis=0
            )


def attend_back(first, count, packed, grad_attended, probs, inverse, delta, left, top, columns, normed, buckets, *deps):
    length, width = grad_attended.shape
    column = pl.BlockSpec((length, 1), lambda g: (0, 0))
    row = pl.BlockSpec((1, length), lambda g: (0, 0))
    return pl.pallas_call(
        functools.partial(attend_back_kernel, first),
        grid=(count,),
        in_specs=[
            pl.BlockSpec((length, 3 * LANES), lambda g: (0, first + g)),
            pl.BlockSpec((length, LANES), lambda g: (0, first + g)),
            pl.BlockSpec((2, length, length // 2), lambda g: (first + g, 0, 0)),
            pl.BlockSpec((2, 1, length), lambda g: (first + g, 0, 0)),
            pl.BlockSpec(delta.shape, lambda g: (0, 0)),
            column, column, row, row,
            pl.BlockSpec((length, width), lambda g: (0, 0)),
            pl.BlockSpec(buckets.shape, lambda g: (0, 0)),
        ] + [pl.BlockSpec(memory_space=pl.ANY)] * len(deps),
        out_specs=[
            pl.BlockSpec((length, 6 * LANES), lambda g: (0, g // 2)),
            pl.BlockSpec((width, 6 * LANES), lambda g: (0, g // 2)),
            pl.BlockSpec((2 * count, 8, LANES), lambda g: (0, 0, 0)),
        ],
        out_shape=[
            jax.ShapeDtypeStruct((length, 3 * LANES * count), BF16),
            jax.ShapeDtypeStruct((width, 3 * LANES * count), BF16),
            jax.ShapeDtypeStruct((2 * count, 8, LANES), F32),
        ],
        scratch_shapes=[
            pltpu.VMEM((2, 64 + 2 * COORDS, length), BF16),
            pltpu.VMEM((length, 2 * COORDS), BF16),
            pltpu.VMEM((2, length, length // 2), BF16),
            pltpu.VMEM((2, 2 * COORDS, length), BF16),
            pltpu.VMEM((TILE, TILE), BF16),
            pltpu.VMEM((width, length), BF16),
            pltpu.VMEM((16 * count, 2 * TILE), F32),
        ],
        compiler_params=pltpu.CompilerParams(vmem_limit_bytes=58 * 1024 * 1024),
        cost_estimate=SMALL,
        name="attend_back",
    )(packed, grad_attended, probs, inverse, delta, columns[1], columns[2], left[None], top[None], normed, buckets, *deps)


ROOT = float(np.sqrt(2.0 / np.pi))


def feed_kernel(width, parts, att_ref, start_ref, up_ref, inner_ref, outer_ref, output_ref, gain_ref,
                middle_ref, act_ref, back_ref, early_ref, late_ref, active, inner_back, normed):
    step = pl.program_id(0)
    length = att_ref.shape[0]
    halves = (slice(0, length // 2), slice(length // 2, length))

    def products(rows):
        return dot(normed[rows], inner_ref[...]), dot(up_ref[rows], outer_ref[...], NT)

    def close(slot, rows, point, reach):
        square = point * point
        bend = jnp.tanh(ROOT * point * (1.0 + 0.044715 * square))
        half = 0.5 + 0.5 * bend
        act = (point * half).astype(BF16)
        slope = half + (0.5 * ROOT) * point * (1.0 - bend * bend) * (1.0 + (3 * 0.044715) * square)
        grads = (slope * reach).astype(BF16)
        act_ref[rows] = act
        back_ref[rows] = grads
        active[slot, rows] = act
        inner_back[slot, rows] = grads

    def body(part):
        goal = late_ref if part == parts else early_ref
        if part == 0:
            for rows in halves:
                middle = start_ref[rows] + dot(att_ref[rows], output_ref[...])
                middle_ref[rows] = middle
                root = lax.rsqrt(jnp.mean(middle * middle, axis=1, keepdims=True) + 1e-06)
                normed[rows] = (middle * root * gain_ref[...]).astype(BF16)
        slot, before = part % 2, (part + 1) % 2
        if part < parts:
            held = products(halves[0])
        if part > 0:
            goal[:, :width] = dot(active[before], up_ref[...], TN).astype(BF16)
        if part < parts:
            close(slot, halves[0], *held)
            held = products(halves[1])
        if part > 0:
            goal[:, width:] = dot(normed[...], inner_back[before], TN).astype(BF16)
        if part < parts:
            close(slot, halves[1], *held)

    for part in range(parts + 1):
        pl.when(step == part)(functools.partial(body, part))


def feed(attended, start, upstream, weights, gain):
    length, width = attended.shape
    parts = weights.shape[1] // width // 2
    once = pl.Buffered(1)
    whole = pl.BlockSpec((length, width), lambda g: (0, 0), pipeline_mode=once)
    column = pl.BlockSpec((length, width), lambda g: (0, jnp.minimum(g, parts - 1)))
    tall = jax.ShapeDtypeStruct((length, parts * width), BF16)
    return pl.pallas_call(
        functools.partial(feed_kernel, width, parts),
        grid=(parts + 1,),
        in_specs=[
            whole, whole, whole,
            pl.BlockSpec((width, width), lambda g: (0, jnp.minimum(g, parts - 1))),
            pl.BlockSpec((width, width), lambda g: (0, parts + jnp.minimum(g, parts - 1))),
            pl.BlockSpec((width, width), lambda g: (0, 2 * parts), pipeline_mode=once),
            pl.BlockSpec((1, width), lambda g: (0, 0)),
        ],
        out_specs=[
            pl.BlockSpec((length, width), lambda g: (0, 0)), column, column,
            pl.BlockSpec((width, 2 * width), lambda g: (0, jnp.clip(g - 1, 0, parts - 2))),
            pl.BlockSpec((width, 2 * width), lambda g: (0, 0)),
        ],
        out_shape=[
            jax.ShapeDtypeStruct((length, width), F32), tall, tall,
            jax.ShapeDtypeStruct((width, 2 * (parts - 1) * width), BF16),
            jax.ShapeDtypeStruct((width, 2 * width), BF16),
        ],
        scratch_shapes=[pltpu.VMEM((2, length, width), BF16)] * 2 + [pltpu.VMEM((length, width), BF16)],
        compiler_params=pltpu.CompilerParams(vmem_limit_bytes=58 * 1024 * 1024),
        cost_estimate=SMALL,
        name="feed",
    )(attended, start, upstream, weights, weights, weights, gain)


def weight_specs(width, parts, places):
    once = pl.Buffered(1)
    specs = [
        pl.BlockSpec((width, parts * width), lambda g: (0, 0), pipeline_mode=once),
        pl.BlockSpec((width, parts * width), lambda g: (0, 1), pipeline_mode=once),
        pl.BlockSpec((width, width), lambda g: (0, 2 * parts), pipeline_mode=once),
        pl.BlockSpec((1, width), lambda g: (0, 0)),
    ]
    return [specs[place] for place in places]


def feed_back_kernel(width, steps, att_ref, middle_ref, up_ref, act_ref, back_ref, inner_ref, outer_ref, output_ref, gain_ref,
                     *rest):
    layer_ref, out_ref, seen_ref, delta_ref, weight_ref, low_middle, attended = rest[-7:]
    step = pl.program_id(0)

    @pl.when(step < steps)
    def _():
        size = att_ref.shape[0]
        rows = pl.ds(pl.multiple_of(step * size, size), size)
        att = att_ref[...]
        attended[rows, :] = att
        gain = gain_ref[...]
        middle = middle_ref[...]
        back = dot(back_ref[...], inner_ref[...], NT)
        result = middle
        for part in range(act_ref.shape[1] // width):
            own = slice(part * width, (part + 1) * width)
            result = result + dot(act_ref[:, own], outer_ref[:, own])
        root = lax.rsqrt(jnp.mean(middle * middle, axis=1, keepdims=True) + 1e-06)
        scaled = middle * root
        slant = jnp.mean(back * scaled * gain, axis=1, keepdims=True)
        grad_middle = up_ref[...].astype(F32) + root * (gain * back - scaled * slant)
        out_ref[...] = grad_middle
        rounded = grad_middle.astype(BF16)
        low_middle[rows, :] = rounded
        layer_ref[...] = result.astype(BF16)
        seen = dot(rounded, output_ref[...], NT).astype(BF16)
        seen_ref[...] = seen
        product = att.astype(F32) * seen.astype(F32)
        high = product.astype(BF16)
        low = (product - high.astype(F32)).astype(BF16)
        head = lax.broadcasted_iota(jnp.int32, (16, width), 0)
        lane = lax.broadcasted_iota(jnp.int32, (16, width), 1)
        marks = jnp.logical_and(lane >= head * 64, lane < head * 64 + 64).astype(F32).astype(BF16)
        delta_ref[...] = dot(marks, high, NT) + dot(marks, low, NT)

    @pl.when(step == steps)
    def _():
        weight_ref[...] = dot(attended[...], low_middle[...], TN).astype(BF16)


def feed_back(attended, middle, upstream, act, back, weights, gain, *deps):
    length, width = attended.shape
    steps = length // TILE
    parts = weights.shape[1] // width // 2
    rows = lambda g: (jnp.minimum(g, steps - 1), 0)
    tile = pl.BlockSpec((TILE, width), rows)
    broad = pl.BlockSpec((TILE, parts * width), rows)
    tokens = jax.ShapeDtypeStruct((length, width), BF16)
    return pl.pallas_call(
        functools.partial(feed_back_kernel, width, steps),
        grid=(steps + 1,),
        in_specs=[tile, tile, tile, broad, broad] + weight_specs(width, parts, (0, 1, 2, 3))
        + [pl.BlockSpec(memory_space=pl.ANY)] * len(deps),
        out_specs=[
            tile, tile, tile,
            pl.BlockSpec((16, TILE), lambda g: (0, jnp.minimum(g, steps - 1))),
            pl.BlockSpec((width, width), lambda g: (0, 0)),
        ],
        out_shape=[
            tokens,
            jax.ShapeDtypeStruct((length, width), F32),
            tokens,
            jax.ShapeDtypeStruct((16, length), F32),
            jax.ShapeDtypeStruct((width, width), BF16),
        ],
        scratch_shapes=[pltpu.VMEM((length, width), BF16)] * 2,
        compiler_params=pltpu.CompilerParams(vmem_limit_bytes=58 * 1024 * 1024),
        cost_estimate=SMALL,
        name="feed_back",
    )(attended, middle, upstream, act, back, weights, weights, weights, gain, *deps)


def last_kernel(start_ref, middle_ref, gain_ref, weight_ref, *rest):
    grads_refs, out_ref = rest[:1], rest[-1]
    start = start_ref[...]
    gain = gain_ref[...]
    root = lax.rsqrt(jnp.mean(start * start, axis=1, keepdims=True) + 1e-06)
    scaled = start * root
    low = 0
    back = 0.0
    for grads_ref in grads_refs:
        high = low + grads_ref.shape[1]
        back = back + dot(grads_ref[...], weight_ref[:, low:high], NT)
        low = high
    slant = jnp.mean(back * scaled * gain, axis=1, keepdims=True)
    out_ref[...] = middle_ref[...] + root * (gain * back - scaled * slant)


def last(start, middle, gain, weights, grads, *deps):
    length, width = start.shape
    tile = pl.BlockSpec((TILE, width), lambda g: (g, 0))
    total = sum(item.shape[1] for item in grads)
    return pl.pallas_call(
        last_kernel,
        grid=(length // TILE,),
        in_specs=[
            tile, tile, pl.BlockSpec((1, width), lambda g: (0, 0)),
            pl.BlockSpec((width, total), lambda g: (0, 0), pipeline_mode=pl.Buffered(1)),
        ]
        + [pl.BlockSpec((TILE, item.shape[1]), lambda g: (g, 0)) for item in grads]
        + [pl.BlockSpec(memory_space=pl.ANY)] * len(deps),
        out_specs=tile,
        out_shape=jax.ShapeDtypeStruct((length, width), F32),
        compiler_params=pltpu.CompilerParams(vmem_limit_bytes=24 * 1024 * 1024),
        cost_estimate=SMALL,
        name="last",
    )(start, middle, gain, weights, *grads, *deps)


def half_kernel(count, core_ref, *refs):
    out_ref = refs[-1]
    low = 0
    for array_ref in refs[:count]:
        high = low + array_ref.shape[-1]
        for place in range(array_ref.shape[0]):
            out_ref[0, place, :, low:high] = array_ref[place, 0, 0]
        low = high


def merge_kernel(count, core_ref, *refs):
    came_ref, out_ref = refs[count], refs[-1]
    low = 0
    for array_ref in refs[:count]:
        high = low + array_ref.shape[-1]
        for place in range(array_ref.shape[0]):
            out_ref[0, place, :, low:high] = (
                array_ref[place, 0, 0].astype(F32) + came_ref[0, place, :, low:high].astype(F32)
            ).astype(BF16)
        low = high


def core_part(kernel, core, arrays, owned, came, *deps):
    outer = arrays[0].shape[0] // owned // 8
    width = sum(array.shape[1] for array in arrays)
    block = pl.BlockSpec((1, outer, owned, width), lambda g, core: (g, 0, 0, 0))
    return pl.pallas_call(
        functools.partial(kernel, len(arrays)),
        grid_spec=pltpu.PrefetchScalarGridSpec(
            num_scalar_prefetch=1,
            grid=(4,),
            in_specs=[
                pl.BlockSpec((outer, 1, 1, owned, array.shape[1]), lambda g, core: (0, g, core[0], 0, 0)) for array in arrays
            ]
            + [block] * len(came) + [pl.BlockSpec(memory_space=pl.ANY)] * len(deps),
            out_specs=block,
        ),
        out_shape=jax.ShapeDtypeStruct((4, outer, owned, width), BF16),
        compiler_params=pltpu.CompilerParams(vmem_limit_bytes=20 * 1024 * 1024),
        cost_estimate=SMALL,
        name="core_part",
    )(core, *[array.reshape(outer, 4, 2, owned, array.shape[1]) for array in arrays], *came, *deps)


def gate_kernel(*refs):
    pass


def gate(array, *deps):
    return pl.pallas_call(
        gate_kernel,
        in_specs=[pl.BlockSpec(memory_space=pl.ANY)] * (1 + len(deps)),
        out_specs=pl.BlockSpec(memory_space=pl.ANY),
        out_shape=jax.ShapeDtypeStruct(array.shape, array.dtype),
        input_output_aliases={0: 0},
        cost_estimate=SMALL,
        name="gate",
    )(array, *deps)


def gather_sum_kernel(array_ref, *rest):
    out_ref = rest[-1]
    total = array_ref[0].astype(F32)
    for place in range(1, array_ref.shape[0]):
        total = total + array_ref[place].astype(F32)
    out_ref[...] = total.astype(out_ref.dtype)


def gather_sum(array, *deps):
    inner, outer, owned, width = array.shape
    return pl.pallas_call(
        gather_sum_kernel,
        grid=(outer,),
        in_specs=[pl.BlockSpec((inner, 1, owned, width), lambda g: (0, g, 0, 0))] + [pl.BlockSpec(memory_space=pl.ANY)] * len(deps),
        out_specs=pl.BlockSpec((1, owned, width), lambda g: (g, 0, 0)),
        out_shape=jax.ShapeDtypeStruct((outer, owned, width), BF16),
        compiler_params=pltpu.CompilerParams(vmem_limit_bytes=20 * 1024 * 1024),
        cost_estimate=SMALL,
        name="gather_sum",
    )(array, *deps)


def finish_kernel(width, level_ref, trio_ref, gain_ref, *out_refs):
    total = level_ref[0].astype(F32)
    for place in range(1, level_ref.shape[0]):
        total = total + level_ref[place].astype(F32)
    out_refs[0][...] = total[:, :width]
    for pair in range(width // LANES):
        for kind in range(3):
            low = width + (3 * pair + kind) * LANES
            out_refs[1 + kind][:, pair * LANES:(pair + 1) * LANES] = total[:, low:low + LANES]
    own = jnp.sum(trio_ref[...].astype(F32) * total[:, width:4 * width], axis=1, keepdims=True)
    out_refs[4][...] = jnp.broadcast_to(own / gain_ref[...].astype(F32), out_refs[4].shape)
    out_refs[5][...] = total[:, 4 * width:]


def finish(level, trio, gain):
    owned, width = trio.shape[0], trio.shape[1] // 3
    square = jax.ShapeDtypeStruct((owned, width), F32)
    return pl.pallas_call(
        functools.partial(finish_kernel, width),
        out_shape=[square] * 4 + [
            jax.ShapeDtypeStruct((owned, LANES), F32),
            jax.ShapeDtypeStruct((owned, level.shape[2] - 4 * width), F32),
        ],
        compiler_params=pltpu.CompilerParams(vmem_limit_bytes=20 * 1024 * 1024),
        cost_estimate=SMALL,
        name="finish",
    )(level, trio, gain)


def weave_kernel(core_ref, own_ref, came_ref, out_ref):
    core = core_ref[0]
    for place in range(own_ref.shape[0]):
        out_ref[0, place, core] = own_ref[place, 0]
        out_ref[0, place, 1 - core] = came_ref[place, 0]


def weave(core, own, came, width):
    inner, outer, owned = own.shape[:3]
    block = pl.BlockSpec((inner, 1, owned, width), lambda g, core: (0, g, 0, 0))
    return pl.pallas_call(
        weave_kernel,
        grid_spec=pltpu.PrefetchScalarGridSpec(
            num_scalar_prefetch=1,
            grid=(outer,),
            in_specs=[block, block],
            out_specs=pl.BlockSpec((1, inner, 2, owned, width), lambda g, core: (g, 0, 0, 0, 0)),
        ),
        out_shape=jax.ShapeDtypeStruct((outer, inner, 2, owned, width), BF16),
        compiler_params=pltpu.CompilerParams(vmem_limit_bytes=20 * 1024 * 1024),
        cost_estimate=SMALL,
        name="weave",
    )(core, own, came)


def turn(array, shift):
    return lax.dynamic_slice_in_dim(jnp.concatenate([array, array], axis=0), shift, array.shape[0], axis=0)


def long_start(segments):
    names = jnp.arange(8, dtype=jnp.int32)
    counts = jnp.sum((segments[None, :] == names[:, None]).astype(jnp.int32), axis=1)
    return jnp.sum((segments < jnp.argmax(counts).astype(jnp.int32)).astype(jnp.int32))


def member_groups(members, low, high):
    apart = 1 << low
    span = 1 << high
    return [
        [base + apart * place for place in range(span // apart)]
        for base in range(members)
        if (base & (span - 1) & ~(apart - 1)) == 0
    ]


def swap_cores(members, array):
    return lax.ppermute(array, "dp", [(place, place ^ 1) for place in range(members)])


def across_plane(members, array):
    return lax.all_to_all(array, "dp", 0, 0, axis_index_groups=member_groups(members, 1, 3))


def along_line(members, array):
    return lax.all_to_all(
        array, "dp", 0, 0, axis_index_groups=member_groups(members, 3, members.bit_length() - 1)
    )


def spread_line(members, array):
    outer = members // 8
    return lax.all_to_all(
        jnp.broadcast_to(array[None], (outer,) + array.shape), "dp", 0, 0,
        axis_index_groups=member_groups(members, 3, members.bit_length() - 1),
    )


def spread_plane(members, array):
    return across_plane(members, jnp.broadcast_to(array[None], (4,) + array.shape))


def per_device(
    members,
    tokens,
    image_features,
    segment_ids,
    box_left,
    box_top,
    cotangent,
    query_weight,
    key_weight,
    value_weight,
    output_weight,
    inner_weight,
    outer_weight,
    attention_gain,
    feed_gain,
    bias_tables,
):
    length, width = tokens.shape[1:]
    owned = query_weight.shape[0]
    parts = inner_weight.shape[1] // width
    spots = bias_tables.shape[0]

    small = jnp.concatenate(
        [
            attention_gain[:, None],
            feed_gain[:, None],
            jnp.pad(bias_tables, (0, 2 * owned - spots)).reshape(owned, 2),
            jnp.zeros((owned, LANES - 4), BF16),
        ],
        axis=1,
    )
    pairs = width // LANES
    trio = jnp.concatenate([query_weight, key_weight, value_weight], axis=1)
    trio = trio.reshape(owned, 3, pairs, LANES).transpose(0, 2, 1, 3).reshape(owned, 3 * width)
    core = (lax.axis_index("dp") & 1).reshape(1)
    inner_own = inner_weight.reshape(owned, width, parts).transpose(0, 2, 1).reshape(owned, parts * width)
    second = lax.all_gather(
        jnp.concatenate([inner_own, outer_weight.reshape(owned, parts * width), output_weight], axis=1),
        "dp", axis=0, tiled=True,
    )
    shift = long_start(segment_ids[0])
    segments, left, top = (turn(item[0], shift) for item in (segment_ids, box_left, box_top))
    start = turn(tokens[0], shift).astype(F32) + turn(image_features[0], shift).astype(F32)
    upstream = turn(cotangent[0], shift)
    root = lax.rsqrt(jnp.mean(start * start, axis=1, keepdims=True) + 1e-06)
    level = spread_line(members, jnp.concatenate([trio, small], axis=1))
    columns = [segments[:, None], left[:, None], top[:, None]]
    part = spread_plane(members, gate(level[:, :, 3 * width:], start, upstream, *columns))
    level = spread_plane(members, level[:, :, :3 * width])
    little = weave(core, part, swap_cores(members, part), LANES).reshape(width, LANES)
    gain_one = little[:, 0].astype(F32)[None]
    gain_two = little[:, 1].astype(F32)[None]
    bands = rows_of(little[:, 2:4].reshape(-1, 2 * owned)[:, :spots].reshape(3 * BUCKETS, HEADS))
    normed = (start * root * gain_one).astype(BF16)
    level = gate(level, upstream, normed, gain_two, bands, *columns)
    project = weave(core, level, swap_cores(members, level), 3 * width).reshape(width, 3 * width)
    scale = jnp.where(jnp.arange(3 * width) % (3 * LANES) < LANES, 0.125, 1.0)[None]
    packed = (dot(normed, project) * scale).astype(BF16)
    attended, probs, inverse = attend(packed, bands, segments, left, top, columns)

    middle, act, inner_back, early, late = feed(attended, start, upstream, second, gain_two)
    early_sum = lax.psum_scatter(early, "dp", scatter_dimension=0, tiled=True)
    sent = core_part(half_kernel, 1 - core, [late], owned, [])
    late_one = core_part(merge_kernel, core, [late], owned, [swap_cores(members, sent)])
    late_two = across_plane(members, late_one)

    layer, grad_middle, grad_attended, delta, output_grad = feed_back(
        attended, middle, upstream, act, inner_back, second, gain_two, late_one
    )
    late_two = gather_sum(late_two, delta)
    late_last = jnp.sum(along_line(members, late_two).astype(F32), axis=0)

    grads, weights, bands_grad = attend_back(
        0, pairs, packed, grad_attended, probs, inverse, delta, left, top, columns, normed, bucket_marks(), late_two
    )
    tables_grad = bands_grad[:, :3, :BUCKETS].transpose(1, 2, 0).reshape(-1)
    room = -(-tables_grad.size // owned // LANES) * LANES
    tables_grad = jnp.pad(tables_grad, (0, owned * room - tables_grad.size)).astype(BF16).reshape(1, owned, room)
    tables_grad = jnp.broadcast_to(tables_grad, (members, owned, room)).reshape(width, room)
    group = [output_grad, weights, tables_grad]
    sent = core_part(half_kernel, 1 - core, group, owned, [], late_last)
    trio_one = core_part(merge_kernel, core, group, owned, [swap_cores(members, sent)])
    trio_two = across_plane(members, trio_one)

    input_gradient = turn(last(start, grad_middle, gain_one, project, [grads], trio_one), length - shift)[None]
    layer = turn(gate(layer, trio_one), length - shift)[None]

    trio_two = gather_sum(trio_two, input_gradient, layer)
    paired = jnp.concatenate([early_sum.astype(F32), late_last], axis=1).reshape(owned, parts, 2, width)
    outer_sum = paired[:, :, 0].reshape(outer_weight.shape)
    inner_sum = paired[:, :, 1].transpose(0, 2, 1).reshape(owned, parts * width)
    feed_gain_grad = jnp.sum(inner_weight.astype(F32) * inner_sum, axis=1) / feed_gain.astype(F32)
    output_sum, query_sum, key_sum, value_sum, gain_grad, tables_last = finish(
        gate(along_line(members, trio_two), inner_sum, outer_sum), trio, attention_gain[:, None]
    )
    tables_last = lax.dynamic_slice_in_dim(tables_last.reshape(-1), lax.axis_index("dp") * spots, spots)
    return (
        layer,
        input_gradient,
        query_sum,
        key_sum,
        value_sum,
        output_sum,
        inner_sum,
        outer_sum,
        gain_grad[:, 0],
        feed_gain_grad,
        tables_last,
    )


def solution(mesh):
    rows = P("dp", None)
    cubes = P("dp", None, None)
    line = P("dp")
    return jax.shard_map(
        functools.partial(per_device, mesh.shape["dp"]),
        mesh=mesh,
        in_specs=(cubes, cubes, rows, rows, rows, cubes) + (rows,) * 6 + (line,) * 3,
        out_specs=(cubes, cubes) + (rows,) * 6 + (line,) * 3,
        check_vma=False,
    )
```

```python
import functools

import numpy as np
import jax
import jax.numpy as jnp
from jax import lax
from jax.sharding import PartitionSpec as P
from jax.experimental import pallas as pl
from jax.experimental.pallas import tpu as pltpu

HEADS = 12
BUCKETS = 32
thresholds = (1, 2, 3, 4, 5, 6, 7, 8, 11, 16, 22, 32, 45, 64, 90)
COORDS = 256
TILE = 256
LANES = 128
AHEAD = 3
SMALL = pl.CostEstimate(flops=10**8, bytes_accessed=10**5, transcendentals=0)
F32 = jnp.float32
BF16 = jnp.bfloat16
NT = (((1,), (1,)), ((), ()))
NN = (((1,), (0,)), ((), ()))
TN = (((0,), (0,)), ((), ()))


def bucket_of(offset):
    magnitude = np.zeros(offset.shape, np.int32)
    for limit in thresholds:
        magnitude = magnitude + (np.abs(offset) >= limit).astype(np.int32)
    return magnitude + BUCKETS // 2 * (offset > 0).astype(np.int32)


def dot(left, right, dims=NN):
    return lax.dot_general(left, right, dims, preferred_element_type=F32)


def rows_of(tables):
    spot = np.arange(2 * TILE)
    signed = np.where(spot < TILE, spot, spot - 2 * TILE)
    marks = np.zeros((3, BUCKETS, 8, 2 * TILE), np.float32)
    picks = ((1, -signed), (2, -signed), (0, -signed), (0, TILE - signed), (0, -TILE - signed))
    for place, (table_index, offset) in enumerate(picks):
        marks[table_index, bucket_of(offset), place, spot] = 1.0
    marks = marks.reshape(3 * BUCKETS, 16 * TILE).astype(BF16)
    return dot(tables, jnp.asarray(marks), TN).reshape(HEADS, 8, 2 * TILE)


def bucket_marks():
    spot = np.arange(2 * TILE)
    falling = TILE - 1 - spot
    rising = spot - (TILE - 1)
    offsets = np.stack([falling, falling, rising, TILE + rising, rising - TILE], axis=1)
    marks = bucket_of(offsets)[:, :, None] == np.arange(LANES)
    return jnp.asarray(marks.astype(BF16).reshape(2 * TILE, 5 * LANES))


def toeplitz(row):
    wide = jnp.broadcast_to(row, (TILE, 2 * TILE))
    return pltpu.roll(wide, 0, axis=1, stride=1, stride_axis=0)[:, :TILE]


def skew_sum(square):
    wide = jnp.concatenate([square, jnp.zeros_like(square)], axis=1)
    return jnp.sum(pltpu.roll(wide, 0, axis=1, stride=1, stride_axis=0), axis=0, keepdims=True)


def one_hot_lanes(column, width):
    return (column == lax.broadcasted_iota(jnp.int32, (column.shape[0], width), 1)).astype(F32).astype(BF16)


def attend_kernel(qkv_ref, band_ref, seg_ref, seg_row, left_ref, top_ref, left_row, top_row, out_ref, probs_ref, sums_ref,
                key_side, query_side, position, marks):
    length = qkv_ref.shape[0]
    half = length // 2

    @pl.when(pl.program_id(0) == 0)
    def _():
        key_side[:, LANES:2 * LANES] = one_hot_lanes(seg_ref[...], LANES)
        key_side[:, 2 * LANES:2 * LANES + COORDS] = one_hot_lanes(left_ref[...], COORDS)
        key_side[:, 2 * LANES + COORDS:] = one_hot_lanes(top_ref[...], COORDS)
        down = lax.broadcasted_iota(jnp.int32, (LANES, length), 0)
        other = jnp.where(jnp.logical_and(down < 8, down != seg_row[...]), F32(-1e30), F32(0)).astype(BF16)
        query_side[0, LANES:2 * LANES, :] = other
        query_side[1, LANES:2 * LANES, :] = other
        down = lax.broadcasted_iota(jnp.int32, (COORDS, length), 0)
        marks[0] = (down == left_row[...]).astype(F32).astype(BF16)
        marks[1] = (down == top_row[...]).astype(F32).astype(BF16)
        query_side[0, 64:LANES, :] = jnp.zeros((64, length), BF16)
        query_side[1, :64, :] = jnp.zeros((64, length), BF16)

    key_side[:, :LANES] = qkv_ref[:, LANES:2 * LANES]
    values_across = qkv_ref[:, 2 * LANES:].T
    queries_across = qkv_ref[:, :LANES].T
    for h in range(2):
        bands = band_ref[h]
        own = slice(h * 64, (h + 1) * 64)
        query_side[h, own, :] = queries_across[own]
        middle, below, above = (toeplitz(bands[t:t + 1]) for t in (2, 3, 4))
        position[h, :TILE, :TILE] = middle
        position[h, TILE:, TILE:] = middle
        position[h, TILE:, :TILE] = below
        position[h, :TILE, TILE:] = above

    for t in range(2):
        low = 2 * LANES + t * COORDS
        grids = jnp.concatenate([toeplitz(band_ref[h, t:t + 1]) for h in range(2)], axis=0).astype(BF16)
        spread = dot(grids, marks[t]).astype(BF16)
        for h in range(2):
            query_side[h, low:low + COORDS, :] = spread[h * COORDS:(h + 1) * COORDS]

    def logits_of(block, tile, h):
        rows = slice(block * half, (block + 1) * half)
        here = slice(block * half + tile * TILE, block * half + (tile + 1) * TILE)
        return dot(key_side[rows, :], query_side[h, :, here]) + position[h, :, tile * TILE:(tile + 1) * TILE]

    def finish(block, tile, h, logits):
        rows = slice(block * half, (block + 1) * half)
        across = slice(tile * TILE, (tile + 1) * TILE)
        here = slice(block * half + tile * TILE, block * half + (tile + 1) * TILE)
        raised = jnp.exp(logits - jnp.max(logits, axis=0, keepdims=True))
        inverse = 1.0 / jnp.sum(raised, axis=0, keepdims=True)
        low = raised.astype(BF16)
        probs_ref[h, rows, across] = low
        sums_ref[h, :, here] = inverse
        return dot(values_across[h * 64:(h + 1) * 64, rows], low) * inverse

    jobs = [(block, tile, h) for block in range(2) for tile in range(half // TILE) for h in range(2)]
    pieces = {}

    def close(job, logits):
        block, tile, h = job
        pieces[job] = finish(*job, logits)
        if h == 1:
            here = slice(block * half + tile * TILE, block * half + (tile + 1) * TILE)
            out_ref[here, :] = jnp.concatenate([pieces[(block, tile, 0)], pieces[(block, tile, 1)]], axis=0).T.astype(BF16)

    waiting = []
    for job in jobs:
        waiting.append((job, logits_of(*job)))
        if len(waiting) > AHEAD:
            close(*waiting.pop(0))
    for item in waiting:
        close(*item)


def attend(packed, bands, seg, left, top, columns):
    length, width = packed.shape[0], packed.shape[1] // 3
    pair = pl.BlockSpec((length, LANES), lambda g: (0, g))
    column = pl.BlockSpec((length, 1), lambda g: (0, 0))
    row = pl.BlockSpec((1, length), lambda g: (0, 0))
    return pl.pallas_call(
        attend_kernel,
        grid=(HEADS // 2,),
        in_specs=[
            pl.BlockSpec((length, 3 * LANES), lambda g: (0, g)),
            pl.BlockSpec((2, 8, 2 * TILE), lambda g: (g, 0, 0)),
            column, row, column, column, row, row,
        ],
        out_specs=[pair, pl.BlockSpec((2, length, length // 2), lambda g: (g, 0, 0)), pl.BlockSpec((2, 1, length), lambda g: (g, 0, 0))],
        out_shape=[
            jax.ShapeDtypeStruct((length, width), BF16),
            jax.ShapeDtypeStruct((HEADS, length, length // 2), BF16),
            jax.ShapeDtypeStruct((HEADS, 1, length), F32),
        ],
        scratch_shapes=[
            pltpu.VMEM((length, 2 * LANES + 2 * COORDS), BF16),
            pltpu.VMEM((2, 2 * LANES + 2 * COORDS, length), BF16),
            pltpu.VMEM((2, length // 2, length // 2), F32),
            pltpu.VMEM((2, COORDS, length), BF16),
        ],
        compiler_params=pltpu.CompilerParams(vmem_limit_bytes=58 * 1024 * 1024),
        cost_estimate=SMALL,
        name="attend",
    )(packed, bands, columns[0], seg[None], columns[1], columns[2], left[None], top[None])


def attend_back_kernel(first, qkv_ref, g_ref, probs_ref, inverse_ref, delta_ref, left_ref, top_ref, left_row, top_row, normed_ref,
                       bucket_ref, *rest):
    grad_ref, weight_ref, band_ref, key_across, marks, low_grads, spread, flip, normed_across, line_sums = rest[-10:]
    length = g_ref.shape[0]
    half = length // 2
    step = pl.program_id(0)

    @pl.when(step == 0)
    def _():
        normed_across[...] = normed_ref[...].T
        marks[:, :COORDS] = one_hot_lanes(left_ref[...], COORDS)
        marks[:, COORDS:] = one_hot_lanes(top_ref[...], COORDS)
        down = COORDS - 1 - lax.broadcasted_iota(jnp.int32, (COORDS, length), 0)
        left_marks = (down == left_row[...]).astype(F32).astype(BF16)
        top_marks = (down == top_row[...]).astype(F32).astype(BF16)
        for h in range(2):
            key_across[h, 64:64 + COORDS, :] = left_marks
            key_across[h, 64 + COORDS:, :] = top_marks
        turned = TILE - 1 - lax.broadcasted_iota(jnp.int32, (TILE, TILE), 0)
        flip[...] = (turned == lax.broadcasted_iota(jnp.int32, (TILE, TILE), 1)).astype(F32).astype(BF16)

    keys_t = qkv_ref[:, LANES:2 * LANES].T
    upper = lax.broadcasted_iota(jnp.int32, (length, LANES), 1) >= LANES // 2
    zero = jnp.zeros((), BF16)
    inverse = jnp.concatenate([inverse_ref[0], inverse_ref[1], jnp.zeros((6, length), F32)], axis=0).T
    grads_h, across_h, queries_h, delta_h = [], [], [], []
    for h in range(2):
        key_across[h, :64, :] = keys_t[h * 64:(h + 1) * 64]
        own = upper == (h == 1)
        mine = jnp.where(own, g_ref[...].astype(F32) * inverse[:, h:h + 1], 0.0).astype(BF16)
        grads_h.append(mine)
        across_h.append(mine.T)
        queries_h.append(jnp.where(own, qkv_ref[:, :LANES], zero))
        delta_h.append(delta_ref[pl.ds(2 * (first + step) + h, 1), :] * inverse_ref[h])
    values = qkv_ref[:, 2 * LANES:]

    def lanes(kind):
        return pl.ds(pl.multiple_of((step % 2) * 3 * LANES + kind * LANES, LANES), LANES)

    def spots(job):
        block, tile, h = job
        return (
            slice(block * half, (block + 1) * half),
            slice(block * half + tile * TILE, block * half + (tile + 1) * TILE),
            slice(tile * TILE, (tile + 1) * TILE),
        )

    def reach_of(job):
        rows, here, _ = spots(job)
        return dot(values[rows], across_h[job[2]][:, here])

    def push(job, reach):
        rows, here, across = spots(job)
        h = job[2]
        grads = (probs_ref[h, rows, across].astype(F32) * (reach - delta_h[h][:, here])).astype(BF16)
        low_grads[h, rows, across] = grads
        return dot(key_across[h, :, rows], grads)

    halves = {}

    def settle(job, both):
        block, tile, h = job
        rows, here, _ = spots(job)
        halves[job] = both[:64] * 0.125
        for t in range(2):
            spread[t, h * COORDS:(h + 1) * COORDS, here] = both[64 + t * COORDS:64 + (t + 1) * COORDS].astype(BF16)
        if h == 1:
            grad_ref[here, lanes(0)] = jnp.concatenate([halves[(block, tile, 0)], halves[job]], axis=0).T.astype(BF16)
        if h == 1 and tile == half // TILE - 1:
            grad_ref[rows, lanes(2)] = (
                dot(probs_ref[0, rows, :], grads_h[0][rows]) + dot(probs_ref[1, rows, :], grads_h[1][rows])
            ).astype(BF16)
            grad_ref[rows, lanes(1)] = (
                dot(low_grads[0, rows, :], queries_h[0][rows]) + dot(low_grads[1, rows, :], queries_h[1][rows])
            ).astype(BF16)

    jobs = [(block, tile, h) for block in range(2) for tile in range(half // TILE) for h in range(2)]
    reaching, pushed = [], []
    for job in jobs + [None] * 3:
        if job is not None:
            reaching.append((job, reach_of(job)))
        if reaching and (job is None or len(reaching) > 1):
            own, reach = reaching.pop(0)
            pushed.append((own, push(own, reach)))
        if pushed and (not reaching or len(pushed) > 1):
            settle(*pushed.pop(0))
    while reaching:
        own, reach = reaching.pop(0)
        pushed.append((own, push(own, reach)))
    while pushed:
        settle(*pushed.pop(0))

    @pl.when(step % 2 == 1)
    def _():
        weight_ref[...] = dot(normed_across[...], grad_ref[...]).astype(BF16)


    def part(h, block, down, tile):
        return low_grads[h, block * half + down * TILE:block * half + (down + 1) * TILE, tile * TILE:(tile + 1) * TILE].astype(F32)

    pressed = [dot(spread[t], marks[:, t * COORDS:(t + 1) * COORDS]) for t in range(2)]
    folded = []
    for h in range(2):
        for square in (
            (part(h, 0, 0, 0) + part(h, 0, 1, 1)) + (part(h, 1, 0, 0) + part(h, 1, 1, 1)),
            part(h, 0, 1, 0) + part(h, 1, 1, 0),
            part(h, 0, 0, 1) + part(h, 1, 0, 1),
        ):
            folded.append(square.astype(BF16))
    turned = dot(jnp.concatenate(folded, axis=0), flip[...])
    for h in range(2):
        squares = [item[h * COORDS:(h + 1) * COORDS] for item in pressed]
        for place in range(3 * h, 3 * h + 3):
            squares.append(turned[place * TILE:(place + 1) * TILE])
        sums = [skew_sum(square) for square in squares]
        line_sums[pl.ds(pl.multiple_of((2 * step + h) * 8, 8), 8), :] = jnp.concatenate(
            sums + [jnp.zeros_like(sums[0])] * 3, axis=0
        )

    @pl.when(step == pl.num_programs(0) - 1)
    def _():
        lines = line_sums[...]
        count = lines.shape[0]
        high = lines.astype(BF16)
        both = dot(jnp.concatenate([high, (lines - high.astype(F32)).astype(BF16)], axis=0), bucket_ref[...])
        both = both[:count] + both[count:]
        for head in range(count // 8):
            picked = [both[head * 8 + t:head * 8 + t + 1, t * LANES:(t + 1) * LANES] for t in range(5)]
            band_ref[head] = jnp.concatenate(
                [picked[2] + picked[3] + picked[4], picked[0], picked[1], jnp.zeros((5, LANES), F32)], axis=0
            )


def attend_back(first, count, packed, grad_attended, probs, inverse, delta, left, top, columns, normed, buckets, *deps):
    length, width = grad_attended.shape
    column = pl.BlockSpec((length, 1), lambda g: (0, 0))
    row = pl.BlockSpec((1, length), lambda g: (0, 0))
    return pl.pallas_call(
        functools.partial(attend_back_kernel, first),
        grid=(count,),
        in_specs=[
            pl.BlockSpec((length, 3 * LANES), lambda g: (0, first + g)),
            pl.BlockSpec((length, LANES), lambda g: (0, first + g)),
            pl.BlockSpec((2, length, length // 2), lambda g: (first + g, 0, 0)),
            pl.BlockSpec((2, 1, length), lambda g: (first + g, 0, 0)),
            pl.BlockSpec(delta.shape, lambda g: (0, 0)),
            column, column, row, row,
            pl.BlockSpec((length, width), lambda g: (0, 0)),
            pl.BlockSpec(buckets.shape, lambda g: (0, 0)),
        ] + [pl.BlockSpec(memory_space=pl.ANY)] * len(deps),
        out_specs=[
            pl.BlockSpec((length, 6 * LANES), lambda g: (0, g // 2)),
            pl.BlockSpec((width, 6 * LANES), lambda g: (0, g // 2)),
            pl.BlockSpec((2 * count, 8, LANES), lambda g: (0, 0, 0)),
        ],
        out_shape=[
            jax.ShapeDtypeStruct((length, 3 * LANES * count), BF16),
            jax.ShapeDtypeStruct((width, 3 * LANES * count), BF16),
            jax.ShapeDtypeStruct((2 * count, 8, LANES), F32),
        ],
        scratch_shapes=[
            pltpu.VMEM((2, 64 + 2 * COORDS, length), BF16),
            pltpu.VMEM((length, 2 * COORDS), BF16),
            pltpu.VMEM((2, length, length // 2), BF16),
            pltpu.VMEM((2, 2 * COORDS, length), BF16),
            pltpu.VMEM((TILE, TILE), BF16),
            pltpu.VMEM((width, length), BF16),
            pltpu.VMEM((16 * count, 2 * TILE), F32),
        ],
        compiler_params=pltpu.CompilerParams(vmem_limit_bytes=58 * 1024 * 1024),
        cost_estimate=SMALL,
        name="attend_back",
    )(packed, grad_attended, probs, inverse, delta, columns[1], columns[2], left[None], top[None], normed, buckets, *deps)


ROOT = float(np.sqrt(2.0 / np.pi))


def feed_kernel(width, parts, att_ref, start_ref, up_ref, inner_ref, outer_ref, output_ref, gain_ref,
                middle_ref, act_ref, back_ref, early_ref, late_ref, active, inner_back, normed):
    step = pl.program_id(0)
    length = att_ref.shape[0]
    halves = (slice(0, length // 2), slice(length // 2, length))

    def products(rows):
        return dot(normed[rows], inner_ref[...]), dot(up_ref[rows], outer_ref[...], NT)

    def close(slot, rows, point, reach):
        square = point * point
        bend = jnp.tanh(ROOT * point * (1.0 + 0.044715 * square))
        half = 0.5 + 0.5 * bend
        act = (point * half).astype(BF16)
        slope = half + (0.5 * ROOT) * point * (1.0 - bend * bend) * (1.0 + (3 * 0.044715) * square)
        grads = (slope * reach).astype(BF16)
        act_ref[rows] = act
        back_ref[rows] = grads
        active[slot, rows] = act
        inner_back[slot, rows] = grads

    def body(part):
        goal = late_ref if part == parts else early_ref
        if part == 0:
            for rows in halves:
                middle = start_ref[rows] + dot(att_ref[rows], output_ref[...])
                middle_ref[rows] = middle
                root = lax.rsqrt(jnp.mean(middle * middle, axis=1, keepdims=True) + 1e-06)
                normed[rows] = (middle * root * gain_ref[...]).astype(BF16)
        slot, before = part % 2, (part + 1) % 2
        if part < parts:
            held = products(halves[0])
        if part > 0:
            goal[:, :width] = dot(active[before], up_ref[...], TN).astype(BF16)
        if part < parts:
            close(slot, halves[0], *held)
            held = products(halves[1])
        if part > 0:
            goal[:, width:] = dot(normed[...], inner_back[before], TN).astype(BF16)
        if part < parts:
            close(slot, halves[1], *held)

    for part in range(parts + 1):
        pl.when(step == part)(functools.partial(body, part))


def feed(attended, start, upstream, weights, gain):
    length, width = attended.shape
    parts = weights.shape[1] // width // 2
    once = pl.Buffered(1)
    whole = pl.BlockSpec((length, width), lambda g: (0, 0), pipeline_mode=once)
    column = pl.BlockSpec((length, width), lambda g: (0, jnp.minimum(g, parts - 1)))
    tall = jax.ShapeDtypeStruct((length, parts * width), BF16)
    return pl.pallas_call(
        functools.partial(feed_kernel, width, parts),
        grid=(parts + 1,),
        in_specs=[
            whole, whole, whole,
            pl.BlockSpec((width, width), lambda g: (0, jnp.minimum(g, parts - 1))),
            pl.BlockSpec((width, width), lambda g: (0, parts + jnp.minimum(g, parts - 1))),
            pl.BlockSpec((width, width), lambda g: (0, 2 * parts), pipeline_mode=once),
            pl.BlockSpec((1, width), lambda g: (0, 0)),
        ],
        out_specs=[
            pl.BlockSpec((length, width), lambda g: (0, 0)), column, column,
            pl.BlockSpec((width, 2 * width), lambda g: (0, jnp.clip(g - 1, 0, parts - 2))),
            pl.BlockSpec((width, 2 * width), lambda g: (0, 0)),
        ],
        out_shape=[
            jax.ShapeDtypeStruct((length, width), F32), tall, tall,
            jax.ShapeDtypeStruct((width, 2 * (parts - 1) * width), BF16),
            jax.ShapeDtypeStruct((width, 2 * width), BF16),
        ],
        scratch_shapes=[pltpu.VMEM((2, length, width), BF16)] * 2 + [pltpu.VMEM((length, width), BF16)],
        compiler_params=pltpu.CompilerParams(vmem_limit_bytes=58 * 1024 * 1024),
        cost_estimate=SMALL,
        name="feed",
    )(attended, start, upstream, weights, weights, weights, gain)


def weight_specs(width, parts, places):
    once = pl.Buffered(1)
    specs = [
        pl.BlockSpec((width, parts * width), lambda g: (0, 0), pipeline_mode=once),
        pl.BlockSpec((width, parts * width), lambda g: (0, 1), pipeline_mode=once),
        pl.BlockSpec((width, width), lambda g: (0, 2 * parts), pipeline_mode=once),
        pl.BlockSpec((1, width), lambda g: (0, 0)),
    ]
    return [specs[place] for place in places]


def feed_back_kernel(width, steps, att_ref, middle_ref, up_ref, act_ref, back_ref, inner_ref, outer_ref, output_ref, gain_ref,
                     *rest):
    layer_ref, out_ref, seen_ref, delta_ref, weight_ref, low_middle, attended = rest[-7:]
    step = pl.program_id(0)

    @pl.when(step < steps)
    def _():
        size = att_ref.shape[0]
        rows = pl.ds(pl.multiple_of(step * size, size), size)
        att = att_ref[...]
        attended[rows, :] = att
        gain = gain_ref[...]
        middle = middle_ref[...]
        back = dot(back_ref[...], inner_ref[...], NT)
        result = middle
        for part in range(act_ref.shape[1] // width):
            own = slice(part * width, (part + 1) * width)
            result = result + dot(act_ref[:, own], outer_ref[:, own])
        root = lax.rsqrt(jnp.mean(middle * middle, axis=1, keepdims=True) + 1e-06)
        scaled = middle * root
        slant = jnp.mean(back * scaled * gain, axis=1, keepdims=True)
        grad_middle = up_ref[...].astype(F32) + root * (gain * back - scaled * slant)
        out_ref[...] = grad_middle
        rounded = grad_middle.astype(BF16)
        low_middle[rows, :] = rounded
        layer_ref[...] = result.astype(BF16)
        seen = dot(rounded, output_ref[...], NT).astype(BF16)
        seen_ref[...] = seen
        product = att.astype(F32) * seen.astype(F32)
        high = product.astype(BF16)
        low = (product - high.astype(F32)).astype(BF16)
        head = lax.broadcasted_iota(jnp.int32, (16, width), 0)
        lane = lax.broadcasted_iota(jnp.int32, (16, width), 1)
        marks = jnp.logical_and(lane >= head * 64, lane < head * 64 + 64).astype(F32).astype(BF16)
        delta_ref[...] = dot(marks, high, NT) + dot(marks, low, NT)

    @pl.when(step == steps)
    def _():
        weight_ref[...] = dot(attended[...], low_middle[...], TN).astype(BF16)


def feed_back(attended, middle, upstream, act, back, weights, gain, *deps):
    length, width = attended.shape
    steps = length // TILE
    parts = weights.shape[1] // width // 2
    rows = lambda g: (jnp.minimum(g, steps - 1), 0)
    tile = pl.BlockSpec((TILE, width), rows)
    broad = pl.BlockSpec((TILE, parts * width), rows)
    tokens = jax.ShapeDtypeStruct((length, width), BF16)
    return pl.pallas_call(
        functools.partial(feed_back_kernel, width, steps),
        grid=(steps + 1,),
        in_specs=[tile, tile, tile, broad, broad] + weight_specs(width, parts, (0, 1, 2, 3))
        + [pl.BlockSpec(memory_space=pl.ANY)] * len(deps),
        out_specs=[
            tile, tile, tile,
            pl.BlockSpec((16, TILE), lambda g: (0, jnp.minimum(g, steps - 1))),
            pl.BlockSpec((width, width), lambda g: (0, 0)),
        ],
        out_shape=[
            tokens,
            jax.ShapeDtypeStruct((length, width), F32),
            tokens,
            jax.ShapeDtypeStruct((16, length), F32),
            jax.ShapeDtypeStruct((width, width), BF16),
        ],
        scratch_shapes=[pltpu.VMEM((length, width), BF16)] * 2,
        compiler_params=pltpu.CompilerParams(vmem_limit_bytes=58 * 1024 * 1024),
        cost_estimate=SMALL,
        name="feed_back",
    )(attended, middle, upstream, act, back, weights, weights, weights, gain, *deps)


def last_kernel(start_ref, middle_ref, gain_ref, weight_ref, *rest):
    grads_refs, out_ref = rest[:1], rest[-1]
    start = start_ref[...]
    gain = gain_ref[...]
    root = lax.rsqrt(jnp.mean(start * start, axis=1, keepdims=True) + 1e-06)
    scaled = start * root
    low = 0
    back = 0.0
    for grads_ref in grads_refs:
        high = low + grads_ref.shape[1]
        back = back + dot(grads_ref[...], weight_ref[:, low:high], NT)
        low = high
    slant = jnp.mean(back * scaled * gain, axis=1, keepdims=True)
    out_ref[...] = middle_ref[...] + root * (gain * back - scaled * slant)


def last(start, middle, gain, weights, grads, *deps):
    length, width = start.shape
    tile = pl.BlockSpec((TILE, width), lambda g: (g, 0))
    total = sum(item.shape[1] for item in grads)
    return pl.pallas_call(
        last_kernel,
        grid=(length // TILE,),
        in_specs=[
            tile, tile, pl.BlockSpec((1, width), lambda g: (0, 0)),
            pl.BlockSpec((width, total), lambda g: (0, 0), pipeline_mode=pl.Buffered(1)),
        ]
        + [pl.BlockSpec((TILE, item.shape[1]), lambda g: (g, 0)) for item in grads]
        + [pl.BlockSpec(memory_space=pl.ANY)] * len(deps),
        out_specs=tile,
        out_shape=jax.ShapeDtypeStruct((length, width), F32),
        compiler_params=pltpu.CompilerParams(vmem_limit_bytes=24 * 1024 * 1024),
        cost_estimate=SMALL,
        name="last",
    )(start, middle, gain, weights, *grads, *deps)


def half_kernel(count, core_ref, *refs):
    out_ref = refs[-1]
    low = 0
    for array_ref in refs[:count]:
        high = low + array_ref.shape[-1]
        for place in range(array_ref.shape[0]):
            out_ref[0, place, :, low:high] = array_ref[place, 0, 0]
        low = high


def merge_kernel(count, core_ref, *refs):
    came_ref, out_ref = refs[count], refs[-1]
    low = 0
    for array_ref in refs[:count]:
        high = low + array_ref.shape[-1]
        for place in range(array_ref.shape[0]):
            out_ref[0, place, :, low:high] = (
                array_ref[place, 0, 0].astype(F32) + came_ref[0, place, :, low:high].astype(F32)
            ).astype(BF16)
        low = high


def core_part(kernel, core, arrays, owned, came, *deps):
    outer = arrays[0].shape[0] // owned // 8
    width = sum(array.shape[1] for array in arrays)
    block = pl.BlockSpec((1, outer, owned, width), lambda g, core: (g, 0, 0, 0))
    return pl.pallas_call(
        functools.partial(kernel, len(arrays)),
        grid_spec=pltpu.PrefetchScalarGridSpec(
            num_scalar_prefetch=1,
            grid=(4,),
            in_specs=[
                pl.BlockSpec((outer, 1, 1, owned, array.shape[1]), lambda g, core: (0, g, core[0], 0, 0)) for array in arrays
            ]
            + [block] * len(came) + [pl.BlockSpec(memory_space=pl.ANY)] * len(deps),
            out_specs=block,
        ),
        out_shape=jax.ShapeDtypeStruct((4, outer, owned, width), BF16),
        compiler_params=pltpu.CompilerParams(vmem_limit_bytes=20 * 1024 * 1024),
        cost_estimate=SMALL,
        name="core_part",
    )(core, *[array.reshape(outer, 4, 2, owned, array.shape[1]) for array in arrays], *came, *deps)


def gate_kernel(*refs):
    pass


def gate(array, *deps):
    return pl.pallas_call(
        gate_kernel,
        in_specs=[pl.BlockSpec(memory_space=pl.ANY)] * (1 + len(deps)),
        out_specs=pl.BlockSpec(memory_space=pl.ANY),
        out_shape=jax.ShapeDtypeStruct(array.shape, array.dtype),
        input_output_aliases={0: 0},
        cost_estimate=SMALL,
        name="gate",
    )(array, *deps)


def gather_sum_kernel(array_ref, *rest):
    out_ref = rest[-1]
    total = array_ref[0].astype(F32)
    for place in range(1, array_ref.shape[0]):
        total = total + array_ref[place].astype(F32)
    out_ref[...] = total.astype(out_ref.dtype)


def gather_sum(array, *deps):
    inner, outer, owned, width = array.shape
    return pl.pallas_call(
        gather_sum_kernel,
        grid=(outer,),
        in_specs=[pl.BlockSpec((inner, 1, owned, width), lambda g: (0, g, 0, 0))] + [pl.BlockSpec(memory_space=pl.ANY)] * len(deps),
        out_specs=pl.BlockSpec((1, owned, width), lambda g: (g, 0, 0)),
        out_shape=jax.ShapeDtypeStruct((outer, owned, width), BF16),
        compiler_params=pltpu.CompilerParams(vmem_limit_bytes=20 * 1024 * 1024),
        cost_estimate=SMALL,
        name="gather_sum",
    )(array, *deps)


def finish_kernel(width, level_ref, trio_ref, gain_ref, *out_refs):
    total = level_ref[0].astype(F32)
    for place in range(1, level_ref.shape[0]):
        total = total + level_ref[place].astype(F32)
    out_refs[0][...] = total[:, :width]
    for pair in range(width // LANES):
        for kind in range(3):
            low = width + (3 * pair + kind) * LANES
            out_refs[1 + kind][:, pair * LANES:(pair + 1) * LANES] = total[:, low:low + LANES]
    own = jnp.sum(trio_ref[...].astype(F32) * total[:, width:4 * width], axis=1, keepdims=True)
    out_refs[4][...] = jnp.broadcast_to(own / gain_ref[...].astype(F32), out_refs[4].shape)
    out_refs[5][...] = total[:, 4 * width:]


def finish(level, trio, gain):
    owned, width = trio.shape[0], trio.shape[1] // 3
    square = jax.ShapeDtypeStruct((owned, width), F32)
    return pl.pallas_call(
        functools.partial(finish_kernel, width),
        out_shape=[square] * 4 + [
            jax.ShapeDtypeStruct((owned, LANES), F32),
            jax.ShapeDtypeStruct((owned, level.shape[2] - 4 * width), F32),
        ],
        compiler_params=pltpu.CompilerParams(vmem_limit_bytes=20 * 1024 * 1024),
        cost_estimate=SMALL,
        name="finish",
    )(level, trio, gain)


def weave_kernel(core_ref, own_ref, came_ref, out_ref):
    core = core_ref[0]
    for place in range(own_ref.shape[0]):
        out_ref[0, place, core] = own_ref[place, 0]
        out_ref[0, place, 1 - core] = came_ref[place, 0]


def weave(core, own, came, width):
    inner, outer, owned = own.shape[:3]
    block = pl.BlockSpec((inner, 1, owned, width), lambda g, core: (0, g, 0, 0))
    return pl.pallas_call(
        weave_kernel,
        grid_spec=pltpu.PrefetchScalarGridSpec(
            num_scalar_prefetch=1,
            grid=(outer,),
            in_specs=[block, block],
            out_specs=pl.BlockSpec((1, inner, 2, owned, width), lambda g, core: (g, 0, 0, 0, 0)),
        ),
        out_shape=jax.ShapeDtypeStruct((outer, inner, 2, owned, width), BF16),
        compiler_params=pltpu.CompilerParams(vmem_limit_bytes=20 * 1024 * 1024),
        cost_estimate=SMALL,
        name="weave",
    )(core, own, came)


def turn(array, shift):
    return lax.dynamic_slice_in_dim(jnp.concatenate([array, array], axis=0), shift, array.shape[0], axis=0)


def long_start(segments):
    names = jnp.arange(8, dtype=jnp.int32)
    counts = jnp.sum((segments[None, :] == names[:, None]).astype(jnp.int32), axis=1)
    return jnp.sum((segments < jnp.argmax(counts).astype(jnp.int32)).astype(jnp.int32))


def member_groups(members, low, high):
    apart = 1 << low
    span = 1 << high
    return [
        [base + apart * place for place in range(span // apart)]
        for base in range(members)
        if (base & (span - 1) & ~(apart - 1)) == 0
    ]


def swap_cores(members, array):
    return lax.ppermute(array, "dp", [(place, place ^ 1) for place in range(members)])


def across_plane(members, array):
    return lax.all_to_all(array, "dp", 0, 0, axis_index_groups=member_groups(members, 1, 3))


def along_line(members, array):
    return lax.all_to_all(
        array, "dp", 0, 0, axis_index_groups=member_groups(members, 3, members.bit_length() - 1)
    )


def spread_line(members, array):
    outer = members // 8
    return lax.all_to_all(
        jnp.broadcast_to(array[None], (outer,) + array.shape), "dp", 0, 0,
        axis_index_groups=member_groups(members, 3, members.bit_length() - 1),
    )


def spread_plane(members, array):
    return across_plane(members, jnp.broadcast_to(array[None], (4,) + array.shape))


def per_device(
    members,
    tokens,
    image_features,
    segment_ids,
    box_left,
    box_top,
    cotangent,
    query_weight,
    key_weight,
    value_weight,
    output_weight,
    inner_weight,
    outer_weight,
    attention_gain,
    feed_gain,
    bias_tables,
):
    length, width = tokens.shape[1:]
    owned = query_weight.shape[0]
    parts = inner_weight.shape[1] // width
    spots = bias_tables.shape[0]

    small = jnp.concatenate(
        [
            attention_gain[:, None],
            feed_gain[:, None],
            jnp.pad(bias_tables, (0, 2 * owned - spots)).reshape(owned, 2),
            jnp.zeros((owned, LANES - 4), BF16),
        ],
        axis=1,
    )
    pairs = width // LANES
    trio = jnp.concatenate([query_weight, key_weight, value_weight], axis=1)
    trio = trio.reshape(owned, 3, pairs, LANES).transpose(0, 2, 1, 3).reshape(owned, 3 * width)
    core = (lax.axis_index("dp") & 1).reshape(1)
    inner_own = inner_weight.reshape(owned, width, parts).transpose(0, 2, 1).reshape(owned, parts * width)
    second = lax.all_gather(
        jnp.concatenate([inner_own, outer_weight.reshape(owned, parts * width), output_weight], axis=1),
        "dp", axis=0, tiled=True,
    )
    shift = long_start(segment_ids[0])
    segments, left, top = (turn(item[0], shift) for item in (segment_ids, box_left, box_top))
    start = turn(tokens[0], shift).astype(F32) + turn(image_features[0], shift).astype(F32)
    upstream = turn(cotangent[0], shift)
    root = lax.rsqrt(jnp.mean(start * start, axis=1, keepdims=True) + 1e-06)
    level = spread_line(members, jnp.concatenate([trio, small], axis=1))
    columns = [segments[:, None], left[:, None], top[:, None]]
    part = spread_plane(members, gate(level[:, :, 3 * width:], start, upstream, *columns))
    level = spread_plane(members, level[:, :, :3 * width])
    little = weave(core, part, swap_cores(members, part), LANES).reshape(width, LANES)
    gain_one = little[:, 0].astype(F32)[None]
    gain_two = little[:, 1].astype(F32)[None]
    bands = rows_of(little[:, 2:4].reshape(-1, 2 * owned)[:, :spots].reshape(3 * BUCKETS, HEADS))
    normed = (start * root * gain_one).astype(BF16)
    level = gate(level, upstream, normed, gain_two, bands, *columns)
    project = weave(core, level, swap_cores(members, level), 3 * width).reshape(width, 3 * width)
    scale = jnp.where(jnp.arange(3 * width) % (3 * LANES) < LANES, 0.125, 1.0)[None]
    packed = (dot(normed, project) * scale).astype(BF16)
    attended, probs, inverse = attend(packed, bands, segments, left, top, columns)

    middle, act, inner_back, early, late = feed(attended, start, upstream, second, gain_two)
    early_sum = lax.psum_scatter(early, "dp", scatter_dimension=0, tiled=True)
    sent = core_part(half_kernel, 1 - core, [late], owned, [])
    late_one = core_part(merge_kernel, core, [late], owned, [swap_cores(members, sent)])
    late_two = across_plane(members, late_one)

    layer, grad_middle, grad_attended, delta, output_grad = feed_back(
        attended, middle, upstream, act, inner_back, second, gain_two, late_one
    )
    late_two = gather_sum(late_two, delta)
    late_last = jnp.sum(along_line(members, late_two).astype(F32), axis=0)

    grads, weights, bands_grad = attend_back(
        0, pairs, packed, grad_attended, probs, inverse, delta, left, top, columns, normed, bucket_marks(), late_two
    )
    tables_grad = bands_grad[:, :3, :BUCKETS].transpose(1, 2, 0).reshape(-1)
    room = -(-tables_grad.size // owned // LANES) * LANES
    tables_grad = jnp.pad(tables_grad, (0, owned * room - tables_grad.size)).astype(BF16).reshape(1, owned, room)
    tables_grad = jnp.broadcast_to(tables_grad, (members, owned, room)).reshape(width, room)
    group = [output_grad, weights, tables_grad]
    sent = core_part(half_kernel, 1 - core, group, owned, [], late_last)
    trio_one = core_part(merge_kernel, core, group, owned, [swap_cores(members, sent)])
    trio_two = across_plane(members, trio_one)

    input_gradient = turn(last(start, grad_middle, gain_one, project, [grads], trio_one), length - shift)[None]
    layer = turn(gate(layer, trio_one), length - shift)[None]

    trio_two = gather_sum(trio_two, input_gradient, layer)
    paired = jnp.concatenate([early_sum.astype(F32), late_last], axis=1).reshape(owned, parts, 2, width)
    outer_sum = paired[:, :, 0].reshape(outer_weight.shape)
    inner_sum = paired[:, :, 1].transpose(0, 2, 1).reshape(owned, parts * width)
    feed_gain_grad = jnp.sum(inner_weight.astype(F32) * inner_sum, axis=1) / feed_gain.astype(F32)
    output_sum, query_sum, key_sum, value_sum, gain_grad, tables_last = finish(
        gate(along_line(members, trio_two), inner_sum, outer_sum), trio, attention_gain[:, None]
    )
    tables_last = lax.dynamic_slice_in_dim(tables_last.reshape(-1), lax.axis_index("dp") * spots, spots)
    return (
        layer,
        input_gradient,
        query_sum,
        key_sum,
        value_sum,
        output_sum,
        inner_sum,
        outer_sum,
        gain_grad[:, 0],
        feed_gain_grad,
        tables_last,
    )


def solution(mesh):
    rows = P("dp", None)
    cubes = P("dp", None, None)
    line = P("dp")
    return jax.shard_map(
        functools.partial(per_device, mesh.shape["dp"]),
        mesh=mesh,
        in_specs=(cubes, cubes, rows, rows, rows, cubes) + (rows,) * 6 + (line,) * 3,
        out_specs=(cubes, cubes) + (rows,) * 6 + (line,) * 3,
        check_vma=False,
    )
```
